32 devices in a mesh: tp: 4 (over y, x), ctx: 2 (over core), outer: 4 (over z).
Axes of the slice: x: 2, y: 2, z: 4, core: 2. Of those that a mesh axis runs over, the one named last changes fastest.
Arguments:
- queries_in: bfloat16 [4096, 2048], P(('outer', 'ctx'), 'tp'), may hold values from -6 to 6
- keys_in: bfloat16 [4096, 2048], P(('outer', 'ctx'), 'tp'), may hold values from -6 to 6
- values_in: bfloat16 [4096, 4096], P(('outer', 'ctx'), 'tp'), may hold values from -6 to 6
- gate_in: bfloat16 [4096, 4096], P(('outer', 'ctx'), 'tp'), may hold values from -6 to 6
- log_decay: float32 [32, 4096], P('tp', ('outer', 'ctx')), may hold values from -1 to 0
- write_strength: float32 [32, 4096], P('tp', ('outer', 'ctx')), may hold values from 0 to 0.95
- doc_lengths: int32 [8], replicated, may hold values from 1 to 32, 64 in all
- norm_gain: float32 [128], replicated, may hold values from 0.1 to 1.9
- out_weight: bfloat16 [4096, 2048], P('tp'), may hold values from -0.09375 to 0.09375
Outputs:
- mixed: bfloat16 [4096, 2048], P(('outer', 'ctx', 'tp'))
The draws below stay inside these ranges and needn't reach their ends.
Inputs may be any that keep to these rules, and one draw needn't show every extreme that they name: `doc_lengths`: the lengths sum to 64, and one document spans 32 stretches.
All inputs are finite; a program needn't handle non-finite values.
Results may differ from the reference program's by a relative error of at most 0.0066.
Values sent between devices are 32-bit elements; how exact they have to be, the bound alone decides.
No kernel may reach another device: no remote copies, remote signals or barrier semaphores. Data moves between devices by JAX's collectives and lax.ppermute only.
A program may use at most 128 MiB of HBM per device.

```python
import math
import jax
import jax.numpy as jnp
import numpy as np
from jax import lax

D = 2048
HK = 16
VALUE_HEADS = 32
DK = 128
DV = 128
STRETCH = 64
DOCS = 8
TOK_DEV = 512
PACKED_TOKENS = 4096


def head_kinds(key):
    share = 0.5
    return jax.random.uniform(jax.random.fold_in(key, 11), (VALUE_HEADS,), jnp.float32) < share


def draw_log_decay(key, part):
    slow_heads = head_kinds(key)
    split_random_keys = jax.random.split(jax.random.fold_in(key, 21), 6)
    slow_rate = jnp.exp(jax.random.uniform(split_random_keys[0], (VALUE_HEADS, 1), jnp.float32, math.log(0.15), math.log(0.6))) * (math.log(10.0) / PACKED_TOKENS)
    fast_rate = jnp.exp(jax.random.uniform(split_random_keys[1], (VALUE_HEADS, 1), jnp.float32, math.log(1.0 / 50.0), math.log(1.0 / 30.0)))
    baseline_decay_rate = jnp.where(slow_heads[:, None], slow_rate, fast_rate)
    per_block_rate = jnp.exp(jax.random.uniform(split_random_keys[2], (VALUE_HEADS, PACKED_TOKENS // TOK_DEV, 1), jnp.float32, math.log(0.5), math.log(2.0)))
    per_block_rate = jnp.broadcast_to(per_block_rate, (VALUE_HEADS, PACKED_TOKENS // TOK_DEV, TOK_DEV)).reshape(VALUE_HEADS, PACKED_TOKENS)
    rate_jitter = jax.random.uniform(split_random_keys[3], (VALUE_HEADS, PACKED_TOKENS), jnp.float32, 0.5, 1.5)
    spike_position = jax.random.randint(split_random_keys[4], (VALUE_HEADS, 3), 0, PACKED_TOKENS)
    spike_mask = jnp.any(jnp.arange(PACKED_TOKENS)[None, :, None] == spike_position[:, None, :], axis=2)
    spike_decay_loss = jax.random.uniform(split_random_keys[5], (VALUE_HEADS, PACKED_TOKENS), jnp.float32, 0.2, 0.5)
    return -(baseline_decay_rate * per_block_rate * rate_jitter) + jnp.where(spike_mask, jnp.log(1.0 - spike_decay_loss), 0.0)


def draw_write_strength(key, part):
    slow_heads = head_kinds(key)
    split_random_keys = jax.random.split(jax.random.fold_in(key, 31), 3)
    slow_level = jnp.minimum(jnp.exp(jax.random.uniform(split_random_keys[0], (VALUE_HEADS, 1), jnp.float32, math.log(0.1), math.log(0.4))) * (8.0 * DK / PACKED_TOKENS), 0.5)
    fast_level = jax.random.uniform(split_random_keys[1], (VALUE_HEADS, 1), jnp.float32, 0.3, 0.7)
    level = jnp.where(slow_heads[:, None], slow_level, fast_level)
    rate_jitter = jax.random.uniform(split_random_keys[2], (VALUE_HEADS, PACKED_TOKENS), jnp.float32, 0.5, 1.5)
    return jnp.minimum(level * rate_jitter, 0.95)


def levels(own_key, dims, pieces, least, high):
    loudness = 1.0
    for position, shards_of in pieces:
        heights = jax.random.uniform(jax.random.fold_in(jax.random.fold_in(own_key, 6), position), (shards_of,), jnp.float32, least / len(pieces), high / len(pieces))
        loudness = loudness * jnp.repeat(jnp.exp(heights), dims[position] // shards_of).reshape((-1,) + (1,) * (len(dims) - 1 - position))
    return loudness


def profile(number_of, total, bound, skew):
    weights = [(1 << 20) // math.isqrt(grade ** skew) + 1 for grade in range(2, number_of + 1)]
    spare, given = total - bound - (number_of - 1), [1] * (number_of - 1)
    while spare > 0:
        candidates = [i for i in range(number_of - 1) if given[i] < bound]
        mass, budget = sum([weights[i] for i in candidates]), spare
        for i in candidates:
            extra = min(bound - given[i], max(1, budget * weights[i] // mass), spare)
            given[i] = given[i] + extra
            spare = spare - extra
    return np.array([bound] + given)


def ragged(rng, count, total, reach, slope):
    if count == 2:
        one = jax.random.randint(rng, (), max(1, total - reach), min(reach, total - 1) + 1)
        return jnp.stack([one, total - one])
    tallies = jnp.asarray(profile(count, total, reach, slope), jnp.int32)
    twos = (count - 1) // 2
    source_of, sink = tallies[1:1 + 2 * twos:2], tallies[2:2 + 2 * twos:2]
    room = jnp.minimum(source_of - 1, reach - sink)
    moved = jax.random.randint(jax.random.fold_in(rng, 1), (twos,), 0, 1 << 20) % (room + 1)
    tallies = tallies.at[1:1 + 2 * twos:2].set(source_of - moved).at[2:2 + 2 * twos:2].set(sink + moved)
    return tallies[jax.random.permutation(jax.random.fold_in(rng, 2), count)]


def centred(key, shape, scale, most, shards=(), held_as=jnp.bfloat16):
    entries = scale * jax.random.normal(key, shape, jnp.float32)
    if shards:
        entries = entries * levels(key, shape, shards, -0.22, 0.18)
    return jnp.clip(entries, -most, most).astype(held_as)


def setup_inputs(seed: int = 0) -> dict:
    seeds = jax.random.split(jax.random.key(seed), 10)
    queries_in = centred(seeds[0], (PACKED_TOKENS, HK * DK), 1.0, 6.0, ((0, 8), (1, 4)))
    keys_in = centred(seeds[1], (PACKED_TOKENS, HK * DK), 1.0, 6.0, ((0, 8), (1, 4)))
    values_in = centred(seeds[2], (PACKED_TOKENS, VALUE_HEADS * DV), 1.0, 6.0, ((0, 8), (1, 4)))
    gate_in = centred(seeds[3], (PACKED_TOKENS, VALUE_HEADS * DV), 1.0, 6.0, ((0, 8), (1, 4)))
    log_decay = draw_log_decay(jax.random.fold_in(seeds[9], 71), 0)
    write_strength = draw_write_strength(jax.random.fold_in(seeds[9], 71), 0)
    doc_lengths = ragged(seeds[6], DOCS, PACKED_TOKENS // STRETCH, PACKED_TOKENS // STRETCH // 2, 1).astype(jnp.int32)
    norm_gain = jnp.clip(1.0 + 0.18 * jax.random.normal(seeds[7], (DV,), jnp.float32), 0.1, 1.9)
    out_weight = centred(seeds[8], (VALUE_HEADS * DV, D), (VALUE_HEADS * DV) ** -0.5, 0.09375, ((0, 4),))
    return dict(queries_in=queries_in, keys_in=keys_in, values_in=values_in, gate_in=gate_in, log_decay=log_decay, write_strength=write_strength, doc_lengths=doc_lengths, norm_gain=norm_gain, out_weight=out_weight)


def unit_norm(rows):
    return rows * lax.rsqrt(lax.optimization_barrier(jnp.sum(rows * rows, axis=-1, keepdims=True)) + 1e-06)

def matmul_heads(left, right):
    return jnp.einsum('...ij,...jk->...ik', left, right, precision=lax.Precision.HIGHEST)

def lower_inverse(strict_part):
    length = strict_part.shape[-1]
    power = -strict_part
    result = jnp.eye(length, dtype=strict_part.dtype) + power
    span = 1
    while 2 * span < length:
        power = matmul_heads(power, power)
        result = result + matmul_heads(result, power)
        span = 2 * span
    return result

def stretch_parts(query_rows, key_rows, value_rows, decay_rows, beta_rows):
    width = key_rows.shape[-1]
    length = decay_rows.shape[-1]
    cumulative = jnp.cumsum(decay_rows, axis=-1)
    order = jnp.arange(length)
    strict = order[:, None] > order[None, :]
    inclusive = order[:, None] >= order[None, :]
    gaps = cumulative[..., :, None] - cumulative[..., None, :]
    decay_strict = jnp.where(strict, jnp.exp(jnp.where(strict, gaps, 0.0)), 0.0)
    decay_incl = jnp.where(inclusive, jnp.exp(jnp.where(inclusive, gaps, 0.0)), 0.0)
    key_gram = jnp.einsum('...id,...jd->...ij', key_rows, key_rows, precision=lax.Precision.HIGHEST)
    strict_part = beta_rows[..., :, None] * key_gram * decay_strict
    right_sides = jnp.concatenate([(beta_rows * jnp.exp(cumulative))[..., None] * key_rows, beta_rows[..., None] * value_rows], axis=-1)
    solved = matmul_heads(lower_inverse(strict_part), right_sides)
    wy_keys = solved[..., :width]
    wy_values = solved[..., width:]
    decayed_query = query_rows * jnp.exp(cumulative)[..., None]
    intra_scores = jnp.einsum('...id,...jd->...ij', query_rows, key_rows, precision=lax.Precision.HIGHEST) * decay_incl
    last_cum = cumulative[..., -1:]
    decayed_keys = key_rows * jnp.exp(last_cum - cumulative)[..., None]
    stretch_decay = jnp.exp(last_cum)
    return (wy_keys, wy_values, decayed_query, intra_scores, decayed_keys, stretch_decay)

def reference(queries_in, keys_in, values_in, gate_in, log_decay, write_strength, doc_lengths, norm_gain, out_weight):
    seq_len = queries_in.shape[0]
    num_stretches = seq_len // STRETCH
    group_size = VALUE_HEADS // HK
    unit_q = unit_norm(queries_in.astype(jnp.float32).reshape(seq_len, HK, DK)).astype(jnp.bfloat16)
    unit_k = unit_norm(keys_in.astype(jnp.float32).reshape(seq_len, HK, DK)).astype(jnp.bfloat16)
    queries = jnp.repeat(unit_q.astype(jnp.float32), group_size, axis=1)
    key_rows = jnp.repeat(unit_k.astype(jnp.float32), group_size, axis=1)
    value_rows = values_in.astype(jnp.float32).reshape(seq_len, VALUE_HEADS, DV)
    starts = jnp.cumsum(doc_lengths).astype(jnp.int32) - doc_lengths
    stretch_ids = jnp.arange(num_stretches, dtype=jnp.int32)
    keep_flags = 1.0 - jnp.any(stretch_ids[:, None] == starts[None, :], axis=1).astype(jnp.float32)

    def blocks(rows):
        return rows.reshape(num_stretches, STRETCH, VALUE_HEADS, rows.shape[-1]).transpose(0, 2, 1, 3)
    decay_blocks = log_decay.reshape(VALUE_HEADS, num_stretches, STRETCH).transpose(1, 0, 2)
    beta_blocks = write_strength.reshape(VALUE_HEADS, num_stretches, STRETCH).transpose(1, 0, 2)

    def advance(state_now, inputs):
        query_rows, key_block, value_block, decay_rows, beta_rows, keep_one = inputs
        wy_keys, wy_values, decayed_query, intra_scores, decayed_keys, stretch_decay = stretch_parts(query_rows, key_block, value_block, decay_rows, beta_rows)
        state_now = state_now * keep_one
        fresh_vals = wy_values - matmul_heads(wy_keys, state_now)
        step_out = matmul_heads(decayed_query, state_now) + matmul_heads(intra_scores, fresh_vals)
        state_now = stretch_decay[..., None] * state_now + jnp.einsum('hcd,hce->hde', decayed_keys, fresh_vals, precision=lax.Precision.HIGHEST)
        return (state_now, step_out)
    state_zero = jnp.zeros((VALUE_HEADS, DK, DV), jnp.float32)
    _, stretch_outs = lax.scan(advance, state_zero, (blocks(queries), blocks(key_rows), blocks(value_rows), decay_blocks, beta_blocks, keep_flags))
    core = stretch_outs.transpose(0, 2, 1, 3).reshape(seq_len, VALUE_HEADS, DV)
    gate_rows = gate_in.astype(jnp.float32).reshape(seq_len, VALUE_HEADS, DV)
    normed = core * lax.rsqrt(lax.optimization_barrier(jnp.mean(core * core, axis=-1, keepdims=True)) + 1e-06)
    gated = (normed * norm_gain * jax.nn.silu(gate_rows)).astype(jnp.bfloat16).reshape(seq_len, VALUE_HEADS * DV)
    return jnp.dot(gated, out_weight, preferred_element_type=jnp.float32).astype(jnp.bfloat16)
```

```python
import functools

import jax
import jax.numpy as jnp
from jax import lax
from jax.experimental import pallas as pl
from jax.experimental.pallas import tpu as pltpu
from jax.sharding import PartitionSpec as P

DK = 128
DV = 128
STRETCH = 64
CHUNK = 2 * STRETCH
F32 = jnp.float32
BF16 = jnp.bfloat16
VMEM_LIMIT = 56 * 1024 * 1024
FAR = 1e30


def mm(left, right):
    return jnp.dot(left, right, preferred_element_type=F32)


def unit_rows(ref, rows):
    raw = ref[rows, :].astype(F32)
    return (raw * lax.rsqrt(jnp.sum(raw * raw, axis=-1, keepdims=True) + 1e-6)).astype(BF16)


def local_kernel(
    chunks, key_heads, place_ref, docs_ref, q_ref, k_ref, v_ref, decay_ref, beta_ref, theirs_ref, mine_ref, reach_ref, core_ref
):
    step = pl.program_id(0)
    key_head = lax.rem(step + place_ref[0], key_heads)
    row = lax.broadcasted_iota(jnp.int32, (CHUNK, CHUNK), 0)
    col = lax.broadcasted_iota(jnp.int32, (CHUNK, CHUNK), 1)
    upper = (row <= col).astype(F32)
    eye = (row == col).astype(F32)
    strict = (row > col).astype(F32)
    crossing = (row >= STRETCH) & (col < STRETCH)
    tri_bias = jnp.where(row >= col, 0.0, -FAR)
    masks = {}
    span = 1
    while span < CHUNK:
        odd_row = lax.rem(row // span, 2) == 1
        masks[span] = (odd_row & (col // span == row // span - 1)).astype(F32).astype(BF16)
        span *= 2
    second = lax.broadcasted_iota(jnp.int32, (1, CHUNK), 1) >= STRETCH
    second_col = lax.broadcasted_iota(jnp.int32, (CHUNK, 1), 0) >= STRETCH

    starts, total = [], jnp.int32(0)
    for j in range(docs_ref.shape[0]):
        starts.append(total)
        total = total + docs_ref[j]

    def keep_flag(stretch):
        here = place_ref[1] * (2 * chunks) + stretch
        hit = here == starts[0]
        for s in starts[1:]:
            hit = hit | (here == s)
        return jnp.where(hit, 0.0, 1.0).astype(F32)

    keeps = [(keep_flag(2 * n), keep_flag(2 * n + 1)) for n in range(chunks)]
    heads_all = decay_ref.shape[0]
    turn = lax.rem(heads_all - 2 * key_head, heads_all)

    units = []
    for n in range(chunks):
        rows = slice(n * CHUNK, (n + 1) * CHUNK)
        k_unit, q_unit = unit_rows(k_ref, rows), unit_rows(q_ref, rows)
        k_turned = k_unit.astype(F32).T.astype(BF16)
        grams = mm(jnp.concatenate([k_unit, q_unit], axis=0), k_turned)
        key_gram, query_gram = grams[:CHUNK], grams[CHUNK:]
        decay = pltpu.roll(decay_ref[:, rows], turn, 0)
        beta = pltpu.roll(beta_ref[:, rows], turn, 0)
        cum = jnp.dot(decay, upper, precision=lax.Precision.HIGHEST, preferred_element_type=F32)
        cum_col, beta_col = cum.T, beta.T
        k1, k2 = keeps[n]
        bias = tri_bias + jnp.where(crossing, (k2 - 1.0) * FAR, 0.0)
        entry = jnp.where(second, k1 * k2, k1)
        leave = jnp.where(second, 1.0, k2)
        entry_col = jnp.where(second_col, k1 * k2, k1)
        for e in range(2):
            c_row, c_col = cum[e : e + 1, :], cum_col[:, e : e + 1]
            b_row = beta[e : e + 1, :]
            fade = jnp.exp((c_col - c_row) + bias)
            noise = (key_gram * fade * beta_col[:, e : e + 1] * strict).astype(BF16)
            last = c_row[:, CHUNK - 1 : CHUNK]
            units.append(
                dict(
                    n=n,
                    e=e,
                    noise=noise,
                    scores=(query_gram * fade).astype(BF16),
                    b_row=b_row,
                    be_row=b_row * jnp.exp(c_row) * entry,
                    q_in=q_unit.astype(F32) * (jnp.exp(c_col) * entry_col),
                    k_out=(k_turned.astype(F32) * (jnp.exp(last - c_row) * leave)).astype(BF16),
                    through=jnp.exp(last) * (k1 * k2),
                    k=k_unit,
                )
            )

    inverses = [eye - (u["noise"] * masks[1]).astype(F32) for u in units]
    span = 2
    while span < CHUNK:
        held = [t.astype(BF16) for t in inverses]
        half = [mm(t, u["noise"] * masks[span]).astype(BF16) for t, u in zip(held, units)]
        inverses = [t - mm(h, b) for t, h, b in zip(inverses, half, held)]
        span *= 2
    outs = []
    for u, t in zip(units, inverses):
        rows = slice(u["n"] * CHUNK, (u["n"] + 1) * CHUNK)
        values = v_ref[rows, u["e"] * DV : (u["e"] + 1) * DV]
        wy_values = mm((t * u["b_row"]).astype(BF16), values)
        wy_keys = mm((t * u["be_row"]).astype(BF16), u["k"])
        pair = jnp.concatenate([wy_keys, wy_values], axis=1).astype(BF16)
        moved = mm(u["k_out"], pair)
        seen = mm(u["scores"], pair)
        outs.append((moved, u["q_in"] - seen[:, :DK], seen[:, DK:], u["through"]))

    for e in range(2):
        cols = slice(e * DV, (e + 1) * DV)
        carried = None
        for n in range(chunks):
            moved, q_eff, own, through = outs[2 * n + e]
            rows = slice(n * CHUNK, (n + 1) * CHUNK)
            if carried is None:
                reach_ref[rows, cols] = q_eff.astype(BF16)
                core_ref[rows, cols] = own
                carried = jnp.concatenate([eye * through - moved[:, :DK], moved[:, DK:]], axis=1)
            else:
                held = carried.astype(BF16)
                read = mm(q_eff.astype(BF16), held)
                reach_ref[rows, cols] = read[:, :DK].astype(BF16)
                core_ref[rows, cols] = read[:, DK:] + own
                step_map = mm(moved[:, :DK].astype(BF16), held)
                carried = carried * through - step_map
                carried = jnp.concatenate([carried[:, :DK], carried[:, DK:] + moved[:, DK:]], axis=1)

        @pl.when(step < key_heads // 2)
        def _():
            theirs_ref[e] = carried

        @pl.when(step >= key_heads // 2)
        def _():
            mine_ref[e] = carried


def local_maps(place, docs, queries, keys, values, decay, beta):
    tokens, key_width = queries.shape
    key_heads = key_width // DK
    heads = decay.shape[0]
    chunks = tokens // CHUNK
    half = key_heads // 2

    def head_block(i, place_ref, docs_ref):
        return (0, lax.rem(i + place_ref[0], key_heads))

    whole = lambda i, place_ref, docs_ref: (0, 0)
    return pl.pallas_call(
        functools.partial(local_kernel, chunks, key_heads),
        out_shape=[
            jax.ShapeDtypeStruct((heads // 2, DK, DK + DV), F32),
            jax.ShapeDtypeStruct((heads // 2, DK, DK + DV), F32),
            jax.ShapeDtypeStruct((tokens, heads * DV), BF16),
            jax.ShapeDtypeStruct((tokens, heads * DV), F32),
        ],
        grid_spec=pltpu.PrefetchScalarGridSpec(
            num_scalar_prefetch=2,
            grid=(key_heads,),
            in_specs=[
                pl.BlockSpec((tokens, DK), head_block),
                pl.BlockSpec((tokens, DK), head_block),
                pl.BlockSpec((tokens, 2 * DV), head_block),
                pl.BlockSpec((heads, tokens), whole),
                pl.BlockSpec((heads, tokens), whole),
            ],
            out_specs=[
                pl.BlockSpec((2, DK, DK + DV), lambda i, p, d: (jnp.minimum(i, half - 1), 0, 0)),
                pl.BlockSpec((2, DK, DK + DV), lambda i, p, d: (jnp.maximum(i - half, 0), 0, 0)),
                pl.BlockSpec((tokens, 2 * DV), head_block),
                pl.BlockSpec((tokens, 2 * DV), head_block),
            ],
        ),
        compiler_params=pltpu.CompilerParams(vmem_limit_bytes=VMEM_LIMIT),
        name="local_maps",
    )(place, docs, queries, keys, values, decay, beta)


def finish_kernel(
    heads, place_ref, reach_ref, core_ref, gate_ref, gain_ref, kept_ref, got_ref, weight_ref,
    send_x_ref, send_y_ref, keep_l_ref, keep_r_ref, gated_ref,
):
    step = pl.program_id(0)
    gain = gain_ref[...]
    first = place_ref[1]
    half = heads // 2
    for side, state_ref in enumerate((kept_ref, got_ref)):
        for j in range(half):
            head = first + j if side == 0 else half - first + j
            cols = pl.ds(pl.multiple_of(head * DV, DV), DV)
            core = core_ref[:, cols] + mm(reach_ref[:, cols], state_ref[j].astype(BF16))
            gate = gate_ref[:, cols].astype(F32)
            normed = core * lax.rsqrt(jnp.mean(core * core, axis=-1, keepdims=True) + 1e-6)
            gated_ref[:, cols] = (normed * gain * (gate / (1.0 + jnp.exp(-gate)))).astype(BF16)
    width = weight_ref.shape[1] // 2
    left = mm(gated_ref[...], weight_ref[:, :width])
    right = mm(gated_ref[...], weight_ref[:, width:])
    for i, (l_ref, l_at, r_ref, r_at) in enumerate(
        (
            (keep_l_ref, 0, keep_r_ref, 0),
            (send_x_ref, 0, keep_r_ref, 1),
            (keep_l_ref, 1, send_y_ref, 0),
            (send_x_ref, 1, send_y_ref, 1),
        )
    ):

        @pl.when(step == i)
        def _(l_ref=l_ref, l_at=l_at, r_ref=r_ref, r_at=r_at):
            l_ref[l_at] = left
            r_ref[r_at] = right


def finish(place, reach, core, gate, gain, kept, got, weight):
    tokens, depth = reach.shape
    width = weight.shape[1] // 2
    heads = depth // DV
    rows = tokens // 4
    row_block = lambda i, place_ref: (i ^ place_ref[0], 0)
    part = jax.ShapeDtypeStruct((2, rows, width), F32)
    part_spec = pl.BlockSpec((2, rows, width), lambda i, p: (0, 0, 0))
    return pl.pallas_call(
        functools.partial(finish_kernel, heads),
        out_shape=[part] * 4,
        grid_spec=pltpu.PrefetchScalarGridSpec(
            num_scalar_prefetch=1,
            grid=(4,),
            in_specs=[
                pl.BlockSpec((rows, depth), row_block),
                pl.BlockSpec((rows, depth), row_block),
                pl.BlockSpec((rows, depth), row_block),
                pl.BlockSpec((1, DV), lambda i, p: (0, 0)),
                pl.BlockSpec(kept.shape, lambda i, p: (0, 0, 0)),
                pl.BlockSpec(got.shape, lambda i, p: (0, 0, 0)),
                pl.BlockSpec(weight.shape, lambda i, p: (0, 0)),
            ],
            out_specs=[part_spec] * 4,
            scratch_shapes=[pltpu.VMEM((rows, depth), BF16)],
        ),
        compiler_params=pltpu.CompilerParams(vmem_limit_bytes=VMEM_LIMIT),
        name="finish",
    )(place, reach, core, gate, gain.reshape(1, DV), kept, got, weight)


def precise(left, right):
    return jnp.einsum("hij,hjk->hik", left, right, precision=lax.Precision.HIGHEST)


def combine(earlier, later):
    joined = precise(later[..., :DK], earlier)
    return jnp.concatenate([joined[..., :DK], joined[..., DK:] + later[..., DK:]], axis=-1)


def apply_map(pair, state):
    return precise(pair[..., :DK], state) + pair[..., DK:]


def group_hops(pair_map, pair_state, outer):
    step = [(i, i + 1) for i in range(outer - 1)]
    state = lax.ppermute(pair_state, "outer", step)
    for _ in range(outer // 2 - 1):
        state = lax.ppermute(precise(pair_map, state) + pair_state, "outer", step)
    return state


def states_before(theirs, mine, ctx, outer):
    here = lax.axis_index("ctx")
    if ctx == 2:
        swap = [(0, 1), (1, 0)]
        other = lax.ppermute(theirs, "ctx", swap)
        is_first = here == 0
        first = jnp.where(is_first, mine, other)
        second = jnp.where(is_first, other, mine)
        group = combine(first, second)
        entering = group_hops(group[..., :DK], group[..., DK:], outer)
        middle = apply_map(first, entering)
        kept = jnp.where(is_first, entering, middle)
        got = lax.ppermute(jnp.where(is_first, middle, entering), "ctx", swap)
        return kept, got
    both = jnp.concatenate([mine, theirs], axis=0)
    blocks = lax.all_gather(both, "ctx")
    identity = jnp.concatenate([jnp.eye(DK, dtype=F32), jnp.zeros((DK, DV), F32)], axis=1)
    start = jnp.broadcast_to(identity, both.shape)

    def hop(k, carry):
        before, through = carry
        through = combine(through, blocks[k])
        return jnp.where(k < here, through, before), through

    before, through = lax.fori_loop(0, ctx, hop, (start, start))
    entering = group_hops(through[..., :DK], through[..., DK:], outer)
    state = apply_map(before, entering)
    half = mine.shape[0]
    return state[:half], state[half:]


def shards(ctx, outer, queries, keys, values, gate, decay, beta, docs, gain, weight):
    heads = decay.shape[0]
    key_heads = queries.shape[1] // DK
    half = key_heads // 2
    here = lax.axis_index("ctx")
    tp_here = lax.axis_index("tp")
    position = lax.axis_index("outer") * ctx + here
    second = here if ctx == 2 else 0 * here
    place = jnp.stack([half * (1 - second), position]).astype(jnp.int32)
    theirs, mine, reach, core = local_maps(place, docs, queries, keys, values, decay, beta)
    kept, got = states_before(theirs, mine, ctx, outer)
    place2 = jnp.stack([tp_here, second * (heads // 2)]).astype(jnp.int32)
    send_x, send_y, keep_l, keep_r = finish(place2, reach, core, gate, gain, kept, got, weight)
    along_x = [(i, i ^ 1) for i in range(4)]
    along_y = [(i, i ^ 2) for i in range(4)]
    got_x = lax.ppermute(send_x, "tp", along_x)
    got_y = lax.ppermute(send_y, "tp", along_y)
    last_l = lax.ppermute(keep_l[1] + got_x[1], "tp", along_y)
    last_r = lax.ppermute(keep_r[1] + got_y[1], "tp", along_x)
    out_l = keep_l[0] + got_x[0] + last_l
    out_r = keep_r[0] + got_y[0] + last_r
    return jnp.concatenate([out_l, out_r], axis=1).astype(BF16)


def solution(mesh):
    ctx, outer = mesh.shape["ctx"], mesh.shape["outer"]
    in_specs = (
        P(("outer", "ctx"), "tp"),
        P(("outer", "ctx"), "tp"),
        P(("outer", "ctx"), "tp"),
        P(("outer", "ctx"), "tp"),
        P("tp", ("outer", "ctx")),
        P("tp", ("outer", "ctx")),
        P(),
        P(),
        P("tp", None),
    )
    out_specs = P(("outer", "ctx", "tp"), None)
    return jax.shard_map(
        functools.partial(shards, ctx, outer), mesh=mesh, in_specs=in_specs, out_specs=out_specs, check_vma=False
    )
```

```python
import functools

import jax
import jax.numpy as jnp
from jax import lax
from jax.experimental import pallas as pl
from jax.experimental.pallas import tpu as pltpu
from jax.sharding import PartitionSpec as P

DK = 128
DV = 128
STRETCH = 64
CHUNK = 2 * STRETCH
F32 = jnp.float32
BF16 = jnp.bfloat16
MIB = 1024 * 1024
MAPS_VMEM = 48 * MIB
READ_VMEM = 12 * MIB
SMALL_VMEM = 4 * MIB
FINISH_VMEM = 16 * MIB
PARTS = (32, 48, 48)
PLACES = 6
FAR = 1e30


def mm(left, right):
    return jnp.dot(left, right, preferred_element_type=F32)


def unit_rows(raw):
    raw = raw.astype(F32)
    return raw * lax.rsqrt(jnp.sum(raw * raw, axis=-1, keepdims=True) + 1e-6)


def corners(left, right):
    nil = jnp.zeros_like(left)
    return jnp.concatenate(
        [jnp.concatenate([left, nil], axis=1), jnp.concatenate([nil, right], axis=1)], axis=0
    )


def doc_starts(place_ref):
    starts, total = [], jnp.int32(0)
    for j in range(PLACES, place_ref.shape[0]):
        starts.append(total)
        total = total + place_ref[j]
    return starts


def chunk_flags(first_stretch, starts, chunks):
    def flag(stretch):
        hit = stretch == starts[0]
        for s in starts[1:]:
            hit = hit | (stretch == s)
        return jnp.where(hit, 0.0, 1.0).astype(F32)

    return [(flag(first_stretch + 2 * n), flag(first_stretch + 2 * n + 1)) for n in range(chunks)]


def fade_bias(row, col, k2):
    crossing = (row >= STRETCH) & (col < STRETCH)
    return jnp.where(row >= col, 0.0, -FAR) + jnp.where(crossing, (k2 - 1.0) * FAR, 0.0)


def maps_kernel(
    chunks, key_heads, place_ref, k_hbm, v_hbm, rates_hbm,
    theirs_ref, mine_ref, pair_t_ref, pair_m_ref, held_t_ref, held_m_ref, cum_t_ref, cum_m_ref,
    k_ref, v_ref, rates_ref, sems,
):
    half = key_heads // 2
    loads = [
        pltpu.make_async_copy(src, dst, sems.at[i])
        for i, (src, dst) in enumerate(
            (
                (rates_hbm, rates_ref),
                (k_hbm, k_ref),
                (v_hbm, v_ref),
            )
        )
    ]
    for load in loads:
        load.start()
    row = lax.broadcasted_iota(jnp.int32, (CHUNK, CHUNK), 0)
    col = lax.broadcasted_iota(jnp.int32, (CHUNK, CHUNK), 1)
    upper = (row <= col).astype(F32)
    eye = (row == col).astype(F32)
    below = (row > col).astype(F32)
    apart = row ^ col
    levels = CHUNK.bit_length() - 1
    masks = [((apart >> level) == 1).astype(F32).astype(BF16) for level in range(levels)]
    second = lax.broadcasted_iota(jnp.int32, (1, CHUNK), 1) >= STRETCH
    both_eye = jnp.concatenate([eye, eye], axis=1)
    loads[0].wait()
    keeps = chunk_flags(place_ref[1] * (2 * chunks), doc_starts(place_ref), chunks)
    heads_all = rates_ref.shape[0] // 2
    loads[1].wait()

    for step in range(2):
        side = lax.rem(step + place_ref[0], 2)
        turn = lax.rem(heads_all - 2 * half * side, heads_all)

        def by_chunk(first):
            rolled = pltpu.roll(rates_ref[first : first + heads_all, :], turn, 0)
            return jnp.concatenate(
                [rolled[:, n * CHUNK : (n + 1) * CHUNK] for n in range(chunks)], axis=0
            )

        decay, beta = by_chunk(0), by_chunk(heads_all)
        cum = jnp.dot(decay, upper, precision=lax.Precision.HIGHEST, preferred_element_type=F32)
        (cum_t_ref if step == 0 else cum_m_ref)[...] = cum
        grown = jnp.exp(cum)
        cum_col, beta_col = cum.T, beta.T

        pairs = []
        for n in range(chunks):
            rows = slice(n * CHUNK, (n + 1) * CHUNK)
            k1, k2 = keeps[n]
            bias = fade_bias(row, col, k2)
            entry = jnp.where(second, k1 * k2, k1)
            leave = jnp.where(second, 1.0, k2)
            for g in range(half):
                key_cols = pl.ds(pl.multiple_of((side * half + g) * DK, DK), DK)
                k_unit = unit_rows(k_ref[rows, key_cols]).astype(BF16)
                k_turned = k_unit.astype(F32).T
                key_gram = mm(k_unit, k_turned.astype(BF16)) * below
                heads = []
                for e in range(2):
                    at = n * heads_all + 2 * g + e
                    c_row, c_col = cum[at : at + 1, :], cum_col[:, at : at + 1]
                    b_row = beta[at : at + 1, :]
                    fade = jnp.exp((c_col - c_row) + bias)
                    last = c_row[:, CHUNK - 1 : CHUNK]
                    heads.append(
                        dict(
                            noise=(key_gram * fade * beta_col[:, at : at + 1]).astype(BF16),
                            b_row=b_row,
                            be_row=b_row * grown[at : at + 1, :] * entry,
                            k_out=(k_turned * (jnp.exp(last - c_row) * leave)).astype(BF16),
                            through=jnp.exp(last) * (k1 * k2),
                        )
                    )
                pairs.append((n, g, k_unit, heads))

        inverses = [
            both_eye - jnp.concatenate([h["noise"] * masks[0] for h in heads], axis=1).astype(F32)
            for _, _, _, heads in pairs
        ]
        for level in range(1, levels):
            held = [t.astype(BF16) for t in inverses]
            part = [
                mm(t, corners(heads[0]["noise"] * masks[level], heads[1]["noise"] * masks[level])).astype(BF16)
                for t, (_, _, _, heads) in zip(held, pairs)
            ]
            inverses = [
                t - mm(p, corners(b[:, :CHUNK], b[:, CHUNK:])) for t, p, b in zip(inverses, part, held)
            ]

        if step == 0:
            loads[2].wait()
        pair_ref, held_ref = ((pair_t_ref, held_t_ref), (pair_m_ref, held_m_ref))[step]
        outs = {}
        for (n, g, k_unit, heads), t in zip(pairs, inverses):
            rows = slice(n * CHUNK, (n + 1) * CHUNK)
            values = v_ref[rows, pl.ds(pl.multiple_of((side * half + g) * 2 * DV, 2 * DV), 2 * DV)]
            b_rows = jnp.concatenate([h["b_row"] for h in heads], axis=1)
            wy_values = mm((t * b_rows).astype(BF16), corners(values[:, :DV], values[:, DV:])).astype(BF16)
            weighted = jnp.concatenate(
                [t[:, e * CHUNK : (e + 1) * CHUNK] * heads[e]["be_row"] for e in range(2)], axis=0
            )
            wy_keys = mm(weighted.astype(BF16), k_unit).astype(BF16)
            for e in range(2):
                pair = jnp.concatenate(
                    [wy_keys[e * CHUNK : (e + 1) * CHUNK], wy_values[:, e * DV : (e + 1) * DV]], axis=1
                )
                pair_ref[2 * g + e, rows, :] = pair
                outs[n, 2 * g + e] = (mm(heads[e]["k_out"], pair), heads[e]["through"])

        carried = [None] * (2 * half)
        for n in range(chunks):
            for j in range(2 * half):
                moved, through = outs[n, j]
                if n == 0:
                    carried[j] = jnp.concatenate([eye * through - moved[:, :DK], moved[:, DK:]], axis=1)
                    continue
                held = carried[j].astype(BF16)
                held_ref[j, n - 1] = held
                after = carried[j] * through - mm(moved[:, :DK].astype(BF16), held)
                carried[j] = jnp.concatenate([after[:, :DK], after[:, DK:] + moved[:, DK:]], axis=1)
        for j in range(2 * half):
            (theirs_ref if step == 0 else mine_ref)[j] = carried[j]


def state_maps(place, keys, values, rates):
    tokens, key_width = keys.shape
    key_heads = key_width // DK
    heads = rates.shape[0] // 2
    chunks = tokens // CHUNK
    part = heads // 2
    local = pl.BlockSpec(memory_space=pltpu.VMEM)
    remote = pl.BlockSpec(memory_space=pltpu.HBM)
    return pl.pallas_call(
        functools.partial(maps_kernel, chunks, key_heads),
        out_shape=[jax.ShapeDtypeStruct((part, DK, DK + DV), F32)] * 2
        + [jax.ShapeDtypeStruct((part, tokens, DK + DV), BF16)] * 2
        + [jax.ShapeDtypeStruct((part, chunks - 1, DK, DK + DV), BF16)] * 2
        + [jax.ShapeDtypeStruct((chunks * heads, CHUNK), F32)] * 2,
        in_specs=[pl.BlockSpec(memory_space=pltpu.SMEM)] + [remote] * 3,
        out_specs=[local] * 8,
        scratch_shapes=[
            pltpu.VMEM(keys.shape, keys.dtype),
            pltpu.VMEM(values.shape, values.dtype),
            pltpu.VMEM(rates.shape, rates.dtype),
            pltpu.SemaphoreType.DMA((3,)),
        ],
        compiler_params=pltpu.CompilerParams(vmem_limit_bytes=MAPS_VMEM),
        name="state_maps",
    )(place, keys, values, rates)


def read_kernel(
    step, chunks, key_heads, place_ref, q_ref, k_ref, cum_ref, pair_ref, held_ref, reach_ref, core_ref
):
    half = key_heads // 2
    side = lax.rem(step + place_ref[0], 2)
    heads_all = 4 * half
    row = lax.broadcasted_iota(jnp.int32, (CHUNK, CHUNK), 0)
    col = lax.broadcasted_iota(jnp.int32, (CHUNK, CHUNK), 1)
    second_col = lax.broadcasted_iota(jnp.int32, (CHUNK, 1), 0) >= STRETCH
    keeps = chunk_flags(place_ref[1] * (2 * chunks), doc_starts(place_ref), chunks)
    cum = cum_ref[...]
    cum_col = cum.T
    grown_col = jnp.exp(cum_col)
    for n in range(chunks):
        rows = slice(n * CHUNK, (n + 1) * CHUNK)
        k1, k2 = keeps[n]
        bias = fade_bias(row, col, k2)
        entry_col = jnp.where(second_col, k1 * k2, k1)
        for g in range(half):
            key_cols = pl.ds(pl.multiple_of((side * half + g) * DK, DK), DK)
            k_unit = unit_rows(k_ref[rows, key_cols]).astype(BF16)
            q_unit = unit_rows(q_ref[rows, key_cols]).astype(BF16)
            query_gram = mm(q_unit, k_unit.astype(F32).T.astype(BF16))
            for e in range(2):
                j = 2 * g + e
                at = n * heads_all + j
                cols = slice(j * DV, (j + 1) * DV)
                fade = jnp.exp((cum_col[:, at : at + 1] - cum[at : at + 1, :]) + bias)
                seen = mm((query_gram * fade).astype(BF16), pair_ref[j, rows, :])
                q_in = q_unit.astype(F32) * (grown_col[:, at : at + 1] * entry_col)
                q_eff = (q_in - seen[:, :DK]).astype(BF16)
                if n == 0:
                    reach_ref[rows, cols] = q_eff
                    core_ref[rows, cols] = seen[:, DK:]
                else:
                    read = mm(q_eff, held_ref[j, n - 1])
                    reach_ref[rows, cols] = read[:, :DK].astype(BF16)
                    core_ref[rows, cols] = read[:, DK:] + seen[:, DK:]


def read_out(step, place, queries, keys, cum, pair, held):
    tokens, key_width = queries.shape
    key_heads = key_width // DK
    chunks = tokens // CHUNK
    local = pl.BlockSpec(memory_space=pltpu.VMEM)
    scalar = pl.BlockSpec(memory_space=pltpu.SMEM)
    width = pair.shape[0] * DV
    return pl.pallas_call(
        functools.partial(read_kernel, step, chunks, key_heads),
        out_shape=[
            jax.ShapeDtypeStruct((tokens, width), BF16),
            jax.ShapeDtypeStruct((tokens, width), F32),
        ],
        in_specs=[scalar] + [local] * 5,
        out_specs=[local] * 2,
        compiler_params=pltpu.CompilerParams(vmem_limit_bytes=READ_VMEM),
        cost_estimate=pl.CostEstimate(flops=2 * 10**9, bytes_accessed=6 * 10**6, transcendentals=10**6),
        name="read_out",
    )(place, queries, keys, cum, pair, held)


def exact(left, right):
    return jnp.dot(left, right, precision=lax.Precision.HIGHEST, preferred_element_type=F32)


def group_kernel(core_ref, mine_ref, other_ref, map_ref, state_ref):
    def join(first_ref, second_ref):
        for j in range(first_ref.shape[0]):
            joined = exact(second_ref[j][:, :DK], first_ref[j])
            map_ref[j] = joined[:, :DK]
            state_ref[j] = joined[:, DK:] + second_ref[j][:, DK:]

    @pl.when(core_ref[2] == 0)
    def _():
        join(mine_ref, other_ref)

    @pl.when(core_ref[2] == 1)
    def _():
        join(other_ref, mine_ref)


def enter_kernel(hops, core_ref, mine_ref, other_ref, former_ref, latter_ref, keep_ref, send_ref):
    early = core_ref[5] < hops

    def through(first_ref, same_ref, out_ref):
        for j in range(first_ref.shape[0]):
            state = jnp.where(early, former_ref[j], latter_ref[j])
            same_ref[j] = state
            out_ref[j] = exact(first_ref[j][:, :DK], state) + first_ref[j][:, DK:]

    @pl.when(core_ref[2] == 0)
    def _():
        through(mine_ref, keep_ref, send_ref)

    @pl.when(core_ref[2] == 1)
    def _():
        through(other_ref, send_ref, keep_ref)


def small_call(kernel, place, *operands):
    part = operands[0].shape[0]
    local = pl.BlockSpec(memory_space=pltpu.VMEM)
    return pl.pallas_call(
        kernel,
        out_shape=[jax.ShapeDtypeStruct((part, DK, DV), F32)] * 2,
        in_specs=[pl.BlockSpec(memory_space=pltpu.SMEM)] + [local] * len(operands),
        out_specs=[local] * 2,
        compiler_params=pltpu.CompilerParams(vmem_limit_bytes=SMALL_VMEM),
    )(place, *operands)


def finish_kernel(
    offset, heads, place_ref, reach_m_ref, core_m_ref, reach_t_ref, core_t_ref, gate_ref, gain_ref, kept_ref, got_ref,
    weight_ref, send_x_ref, send_y_ref, keep_l_ref, keep_r_ref, gated_ref,
):
    size = send_x_ref.shape[1]
    share = gate_ref.shape[0] // 4
    gain = gain_ref[...]
    first = place_ref[4]
    half = heads // 2
    for i in range(4):
        rows = pl.ds(pl.multiple_of((i ^ place_ref[3]) * share + offset, 16), size)
        for side, (reach_ref, core_ref, state_ref) in enumerate(
            ((reach_m_ref, core_m_ref, kept_ref), (reach_t_ref, core_t_ref, got_ref))
        ):
            for j in range(half):
                head = first + j if side == 0 else half - first + j
                cols = pl.ds(pl.multiple_of(head * DV, DV), DV)
                own = slice(j * DV, (j + 1) * DV)
                core = core_ref[rows, own] + mm(reach_ref[rows, own], state_ref[j].astype(BF16))
                gate = gate_ref[rows, cols].astype(F32)
                normed = core * lax.rsqrt(jnp.mean(core * core, axis=-1, keepdims=True) + 1e-6)
                gated = normed * gain * (gate / (1.0 + jnp.exp(-gate)))
                gated_ref[i * size : (i + 1) * size, cols] = gated.astype(BF16)
    width = weight_ref.shape[1] // 2
    left = mm(gated_ref[...], weight_ref[:, :width])
    right = mm(gated_ref[...], weight_ref[:, width:])
    for i, (l_ref, l_at, r_ref, r_at) in enumerate(
        (
            (keep_l_ref, 0, keep_r_ref, 0),
            (send_x_ref, 0, keep_r_ref, 1),
            (keep_l_ref, 1, send_y_ref, 0),
            (send_x_ref, 1, send_y_ref, 1),
        )
    ):
        l_ref[l_at] = left[i * size : (i + 1) * size]
        r_ref[r_at] = right[i * size : (i + 1) * size]


def finish(offset, size, place, reads, gate, gain, kept, got, weight):
    depth = gate.shape[1]
    width = weight.shape[1] // 2
    heads = depth // DV
    local = pl.BlockSpec(memory_space=pltpu.VMEM)
    return pl.pallas_call(
        functools.partial(finish_kernel, offset, heads),
        out_shape=[jax.ShapeDtypeStruct((2, size, width), F32)] * 4,
        in_specs=[pl.BlockSpec(memory_space=pltpu.SMEM)] + [local] * 9,
        out_specs=[local] * 4,
        scratch_shapes=[pltpu.VMEM((4 * size, depth), BF16)],
        compiler_params=pltpu.CompilerParams(vmem_limit_bytes=FINISH_VMEM),
        cost_estimate=pl.CostEstimate(
            flops=8 * size * depth * width * 2, bytes_accessed=16 * size * width, transcendentals=4 * size * depth
        ),
        name="finish",
    )(place, *reads, gate, gain.reshape(1, DV), kept, got, weight)


def precise(left, right):
    return jnp.einsum("hij,hjk->hik", left, right, precision=lax.Precision.HIGHEST)


def combine(earlier, later):
    joined = precise(later[..., :DK], earlier)
    return jnp.concatenate([joined[..., :DK], joined[..., DK:] + later[..., DK:]], axis=-1)


def apply_map(pair, state):
    return precise(pair[..., :DK], state) + pair[..., DK:]


def group_hops(pair_map, pair_state, outer, beside=()):
    results, arrivals = [], []
    leaving = pair_state
    for hop in range(outer // 2):
        step = [(i, i + 1) for i in range(hop, outer - 1)] + [(outer - 1, hop)]
        state = lax.ppermute(leaving, "outer", step)
        if hop < len(beside):
            call, place, rest = beside[hop]
            place, _ = lax.optimization_barrier((place, leaving))
            result = call(place, *rest)
            state, result = lax.optimization_barrier((state, result))
            results.append(result)
        arrivals.append(state)
        if hop < outer // 2 - 1:
            if hop:
                state = jnp.where(lax.axis_index("outer") <= hop, arrivals[-2], state)
                arrivals[-1] = state
            leaving = precise(pair_map, state) + pair_state
    return arrivals[-2], arrivals[-1], results


def whole_prefix(mine, theirs, ctx, outer):
    here = lax.axis_index("ctx")
    both = jnp.concatenate([mine, theirs], axis=0)
    blocks = lax.all_gather(both, "ctx")
    identity = jnp.concatenate([jnp.eye(DK, dtype=F32), jnp.zeros((DK, DV), F32)], axis=1)
    start = jnp.broadcast_to(identity, both.shape)

    def hop(k, carry):
        before, through = carry
        through = combine(through, blocks[k])
        return jnp.where(k < here, through, before), through

    before, through = lax.fori_loop(0, ctx, hop, (start, start))
    former, latter, _ = group_hops(through[..., :DK], through[..., DK:], outer)
    entering = jnp.where(lax.axis_index("outer") < outer // 2, former, latter)
    state = apply_map(before, entering)
    half = mine.shape[0]
    return state[:half], state[half:]


def shards(ctx, outer, queries, keys, values, gate, decay, beta, docs, gain, weight):
    heads = decay.shape[0]
    here = lax.axis_index("ctx")
    position = lax.axis_index("outer") * ctx + here
    second = here if ctx == 2 else 0 * here
    group = lax.axis_index("outer")
    place = jnp.stack([1 - second, position, here, lax.axis_index("tp"), second * (heads // 2), group])
    place = jnp.concatenate([place.astype(jnp.int32), docs])
    rates = jnp.concatenate([decay, beta], axis=0)
    theirs, mine, pair_t, pair_m, held_t, held_m, cum_t, cum_m = state_maps(place, keys, values, rates)
    if ctx == 2:
        swap = [(0, 1), (1, 0)]
        other = lax.ppermute(theirs, "ctx", swap)
        group_map, group_state = small_call(group_kernel, place, mine, other)
        beside = (
            (functools.partial(read_out, 1), place, (queries, keys, cum_m, pair_m, held_m)),
            (functools.partial(read_out, 0), place, (queries, keys, cum_t, pair_t, held_t)),
        )
        former, latter, reads = group_hops(group_map, group_state, outer, beside)
        kept, sent = small_call(functools.partial(enter_kernel, outer // 2), place, mine, other, former, latter)
        got = lax.ppermute(sent, "ctx", swap)
    else:
        kept, got = whole_prefix(mine, theirs, ctx, outer)
        reads = [
            read_out(1, place, queries, keys, cum_m, pair_m, held_m),
            read_out(0, place, queries, keys, cum_t, pair_t, held_t),
        ]
    reads = [array for pair in reads for array in pair]
    along_x = [(i, i ^ 1) for i in range(4)]
    along_y = [(i, i ^ 2) for i in range(4)]
    halves, offset = [], 0
    for size in PARTS:
        send_x, send_y, keep_l, keep_r = finish(offset, size, place, reads, gate, gain, kept, got, weight)
        offset += size
        got_x = lax.ppermute(send_x, "tp", along_x)
        got_y = lax.ppermute(send_y, "tp", along_y)
        halves.append((keep_l, keep_r, got_x, got_y))
    outs = []
    for keep_l, keep_r, got_x, got_y in halves:
        last_l = lax.ppermute(keep_l[1] + got_x[1], "tp", along_y)
        last_r = lax.ppermute(keep_r[1] + got_y[1], "tp", along_x)
        out_l = keep_l[0] + got_x[0] + last_l
        out_r = keep_r[0] + got_y[0] + last_r
        outs.append(jnp.concatenate([out_l, out_r], axis=1).astype(BF16))
    return jnp.concatenate(outs, axis=0)


def solution(mesh):
    ctx, outer = mesh.shape["ctx"], mesh.shape["outer"]
    in_specs = (
        P(("outer", "ctx"), "tp"),
        P(("outer", "ctx"), "tp"),
        P(("outer", "ctx"), "tp"),
        P(("outer", "ctx"), "tp"),
        P("tp", ("outer", "ctx")),
        P("tp", ("outer", "ctx")),
        P(),
        P(),
        P("tp", None),
    )
    out_specs = P(("outer", "ctx", "tp"), None)
    return jax.shard_map(
        functools.partial(shards, ctx, outer), mesh=mesh, in_specs=in_specs, out_specs=out_specs, check_vma=False
    )
```

```python
import functools

import jax
import jax.numpy as jnp
from jax import lax
from jax.experimental import pallas as pl
from jax.experimental.pallas import tpu as pltpu
from jax.sharding import PartitionSpec as P

DK = 128
DV = 128
STRETCH = 64
CHUNK = 2 * STRETCH
F32 = jnp.float32
BF16 = jnp.bfloat16
MIB = 1024 * 1024
MAPS_VMEM = 48 * MIB
READ_VMEM = 12 * MIB
SMALL_VMEM = 4 * MIB
FINISH_VMEM = 16 * MIB
PARTS = (32, 48, 48)
DOC_ROWS = 8
FAR = 1e30


def mm(left, right):
    return jnp.dot(left, right, preferred_element_type=F32)


def unit_rows(raw):
    raw = raw.astype(F32)
    return raw * lax.rsqrt(jnp.sum(raw * raw, axis=-1, keepdims=True) + 1e-6)


def corners(left, right):
    nil = jnp.zeros_like(left)
    return jnp.concatenate(
        [jnp.concatenate([left, nil], axis=1), jnp.concatenate([nil, right], axis=1)], axis=0
    )


def keep_flags(docs, first_stretch, stretches):
    before = lax.broadcasted_iota(jnp.int32, (CHUNK, CHUNK), 0) < lax.broadcasted_iota(jnp.int32, (CHUNK, CHUNK), 1)
    starts = mm(docs.astype(BF16), before.astype(F32).astype(BF16))[0:1, :]
    ids = (lax.broadcasted_iota(jnp.int32, (stretches, CHUNK), 0) + first_stretch).astype(F32)
    return 1.0 - jnp.max(jnp.where(ids == starts, 1.0, 0.0), axis=1, keepdims=True)


def fade_bias(row, col, k2):
    crossing = (row >= STRETCH) & (col < STRETCH)
    return jnp.where(row >= col, 0.0, -FAR) + jnp.where(crossing, (k2 - 1.0) * FAR, 0.0)


def maps_kernel(
    chunks, key_heads, place_ref, k_hbm, v_hbm, rates_hbm,
    theirs_ref, mine_ref, pair_t_ref, pair_m_ref, held_t_ref, held_m_ref, cum_t_ref, cum_m_ref,
    k_ref, v_ref, rates_ref, sems,
):
    half = key_heads // 2
    loads = [
        pltpu.make_async_copy(src, dst, sems.at[i])
        for i, (src, dst) in enumerate(
            (
                (rates_hbm, rates_ref),
                (k_hbm, k_ref),
                (v_hbm, v_ref),
            )
        )
    ]
    for load in loads:
        load.start()
    row = lax.broadcasted_iota(jnp.int32, (CHUNK, CHUNK), 0)
    col = lax.broadcasted_iota(jnp.int32, (CHUNK, CHUNK), 1)
    upper = (row <= col).astype(F32)
    eye = (row == col).astype(F32)
    below = (row > col).astype(F32)
    apart = row ^ col
    levels = CHUNK.bit_length() - 1
    masks = [((apart >> level) == 1).astype(F32).astype(BF16) for level in range(levels)]
    second = lax.broadcasted_iota(jnp.int32, (1, CHUNK), 1) >= STRETCH
    both_eye = jnp.concatenate([eye, eye], axis=1)
    loads[0].wait()
    heads_all = (rates_ref.shape[0] - DOC_ROWS) // 2
    keep = keep_flags(rates_ref[2 * heads_all :, :CHUNK], place_ref[1] * (2 * chunks), 2 * chunks)
    keeps = [(keep[2 * n : 2 * n + 1], keep[2 * n + 1 : 2 * n + 2]) for n in range(chunks)]
    loads[1].wait()

    outs = {}
    for step in range(2):
        side = lax.rem(step + place_ref[0], 2)
        turn = lax.rem(heads_all - 2 * half * side, heads_all)

        def by_chunk(first):
            rolled = pltpu.roll(rates_ref[first : first + heads_all, :], turn, 0)
            return jnp.concatenate(
                [rolled[:, n * CHUNK : (n + 1) * CHUNK] for n in range(chunks)], axis=0
            )

        decay, beta = by_chunk(0), by_chunk(heads_all)
        cum = jnp.dot(decay, upper, precision=lax.Precision.HIGHEST, preferred_element_type=F32)
        cum_ref = (cum_t_ref, cum_m_ref)[step]
        cum_ref[: chunks * heads_all, :] = cum
        cum_ref[chunks * heads_all :, :] = jnp.broadcast_to(keep, (2 * chunks, CHUNK))
        grown = jnp.exp(cum)
        cum_col, beta_col = cum.T, beta.T

        pairs = []
        for n in range(chunks):
            rows = slice(n * CHUNK, (n + 1) * CHUNK)
            k1, k2 = keeps[n]
            bias = fade_bias(row, col, k2)
            entry = jnp.where(second, k1 * k2, k1)
            leave = jnp.where(second, 1.0, k2)
            for g in range(half):
                key_cols = pl.ds(pl.multiple_of((side * half + g) * DK, DK), DK)
                k_unit = unit_rows(k_ref[rows, key_cols]).astype(BF16)
                k_turned = k_unit.astype(F32).T
                key_gram = mm(k_unit, k_turned.astype(BF16)) * below
                heads = []
                for e in range(2):
                    at = n * heads_all + 2 * g + e
                    c_row, c_col = cum[at : at + 1, :], cum_col[:, at : at + 1]
                    b_row = beta[at : at + 1, :]
                    fade = jnp.exp((c_col - c_row) + bias)
                    last = c_row[:, CHUNK - 1 : CHUNK]
                    heads.append(
                        dict(
                            noise=(key_gram * fade * beta_col[:, at : at + 1]).astype(BF16),
                            b_row=b_row,
                            be_row=b_row * grown[at : at + 1, :] * entry,
                            k_out=(k_turned * (jnp.exp(last - c_row) * leave)).astype(BF16),
                            through=jnp.exp(last) * (k1 * k2),
                        )
                    )
                pairs.append((n, g, k_unit, heads))

        inverses = [
            both_eye - jnp.concatenate([h["noise"] * masks[0] for h in heads], axis=1).astype(F32)
            for _, _, _, heads in pairs
        ]
        for level in range(1, levels):
            held = [t.astype(BF16) for t in inverses]
            part = [
                mm(t, corners(heads[0]["noise"] * masks[level], heads[1]["noise"] * masks[level])).astype(BF16)
                for t, (_, _, _, heads) in zip(held, pairs)
            ]
            inverses = [
                t - mm(p, corners(b[:, :CHUNK], b[:, CHUNK:])) for t, p, b in zip(inverses, part, held)
            ]

        if step == 0:
            loads[2].wait()
        pair_ref = (pair_t_ref, pair_m_ref)[step]
        for (n, g, k_unit, heads), t in zip(pairs, inverses):
            rows = slice(n * CHUNK, (n + 1) * CHUNK)
            values = v_ref[rows, pl.ds(pl.multiple_of((side * half + g) * 2 * DV, 2 * DV), 2 * DV)]
            b_rows = jnp.concatenate([h["b_row"] for h in heads], axis=1)
            wy_values = mm((t * b_rows).astype(BF16), corners(values[:, :DV], values[:, DV:])).astype(BF16)
            weighted = jnp.concatenate(
                [t[:, e * CHUNK : (e + 1) * CHUNK] * heads[e]["be_row"] for e in range(2)], axis=0
            )
            wy_keys = mm(weighted.astype(BF16), k_unit).astype(BF16)
            for e in range(2):
                pair = jnp.concatenate(
                    [wy_keys[e * CHUNK : (e + 1) * CHUNK], wy_values[:, e * DV : (e + 1) * DV]], axis=1
                )
                pair_ref[2 * g + e, rows, :] = pair
                outs[step, n, 2 * g + e] = (mm(heads[e]["k_out"], pair), heads[e]["through"])

    carried = {}
    for n in range(chunks):
        for step in range(2):
            for j in range(2 * half):
                moved, through = outs[step, n, j]
                if n == 0:
                    carried[step, j] = jnp.concatenate([eye * through - moved[:, :DK], moved[:, DK:]], axis=1)
                    continue
                held = carried[step, j].astype(BF16)
                (held_t_ref, held_m_ref)[step][j, n - 1] = held
                after = carried[step, j] * through - mm(moved[:, :DK].astype(BF16), held)
                carried[step, j] = jnp.concatenate([after[:, :DK], after[:, DK:] + moved[:, DK:]], axis=1)
    for j in range(2 * half):
        theirs_ref[j] = carried[0, j]
        mine_ref[j] = carried[1, j]


def state_maps(place, keys, values, rates):
    tokens, key_width = keys.shape
    key_heads = key_width // DK
    heads = (rates.shape[0] - DOC_ROWS) // 2
    chunks = tokens // CHUNK
    part = heads // 2
    local = pl.BlockSpec(memory_space=pltpu.VMEM)
    remote = pl.BlockSpec(memory_space=pltpu.HBM)
    return pl.pallas_call(
        functools.partial(maps_kernel, chunks, key_heads),
        out_shape=[jax.ShapeDtypeStruct((part, DK, DK + DV), F32)] * 2
        + [jax.ShapeDtypeStruct((part, tokens, DK + DV), BF16)] * 2
        + [jax.ShapeDtypeStruct((part, chunks - 1, DK, DK + DV), BF16)] * 2
        + [jax.ShapeDtypeStruct((chunks * (heads + 2), CHUNK), F32)] * 2,
        in_specs=[pl.BlockSpec(memory_space=pltpu.SMEM)] + [remote] * 3,
        out_specs=[local] * 8,
        scratch_shapes=[
            pltpu.VMEM(keys.shape, keys.dtype),
            pltpu.VMEM(values.shape, values.dtype),
            pltpu.VMEM(rates.shape, rates.dtype),
            pltpu.SemaphoreType.DMA((3,)),
        ],
        compiler_params=pltpu.CompilerParams(vmem_limit_bytes=MAPS_VMEM),
        name="state_maps",
    )(place, keys, values, rates)


def read_kernel(
    step, chunks, key_heads, place_ref, q_ref, k_ref, cum_ref, pair_ref, held_ref, reach_ref, core_ref
):
    half = key_heads // 2
    side = lax.rem(step + place_ref[0], 2)
    heads_all = 4 * half
    row = lax.broadcasted_iota(jnp.int32, (CHUNK, CHUNK), 0)
    col = lax.broadcasted_iota(jnp.int32, (CHUNK, CHUNK), 1)
    second_col = lax.broadcasted_iota(jnp.int32, (CHUNK, 1), 0) >= STRETCH
    keep = cum_ref[chunks * heads_all :, :]
    keeps = [(keep[2 * n : 2 * n + 1, 0:1], keep[2 * n + 1 : 2 * n + 2, 0:1]) for n in range(chunks)]
    cum = cum_ref[: chunks * heads_all, :]
    cum_col = cum.T
    grown_col = jnp.exp(cum_col)
    for n in range(chunks):
        rows = slice(n * CHUNK, (n + 1) * CHUNK)
        k1, k2 = keeps[n]
        bias = fade_bias(row, col, k2)
        entry_col = jnp.where(second_col, k1 * k2, k1)
        for g in range(half):
            key_cols = pl.ds(pl.multiple_of((side * half + g) * DK, DK), DK)
            k_unit = unit_rows(k_ref[rows, key_cols]).astype(BF16)
            q_unit = unit_rows(q_ref[rows, key_cols]).astype(BF16)
            query_gram = mm(q_unit, k_unit.astype(F32).T.astype(BF16))
            for e in range(2):
                j = 2 * g + e
                at = n * heads_all + j
                cols = slice(j * DV, (j + 1) * DV)
                fade = jnp.exp((cum_col[:, at : at + 1] - cum[at : at + 1, :]) + bias)
                seen = mm((query_gram * fade).astype(BF16), pair_ref[j, rows, :])
                q_in = q_unit.astype(F32) * (grown_col[:, at : at + 1] * entry_col)
                q_eff = (q_in - seen[:, :DK]).astype(BF16)
                if n == 0:
                    reach_ref[rows, cols] = q_eff
                    core_ref[rows, cols] = seen[:, DK:]
                else:
                    read = mm(q_eff, held_ref[j, n - 1])
                    reach_ref[rows, cols] = read[:, :DK].astype(BF16)
                    core_ref[rows, cols] = read[:, DK:] + seen[:, DK:]


def read_out(step, place, queries, keys, cum, pair, held):
    tokens, key_width = queries.shape
    key_heads = key_width // DK
    chunks = tokens // CHUNK
    local = pl.BlockSpec(memory_space=pltpu.VMEM)
    scalar = pl.BlockSpec(memory_space=pltpu.SMEM)
    width = pair.shape[0] * DV
    return pl.pallas_call(
        functools.partial(read_kernel, step, chunks, key_heads),
        out_shape=[
            jax.ShapeDtypeStruct((tokens, width), BF16),
            jax.ShapeDtypeStruct((tokens, width), F32),
        ],
        in_specs=[scalar] + [local] * 5,
        out_specs=[local] * 2,
        compiler_params=pltpu.CompilerParams(vmem_limit_bytes=READ_VMEM),
        cost_estimate=pl.CostEstimate(flops=2 * 10**9, bytes_accessed=6 * 10**6, transcendentals=10**6),
        name="read_out",
    )(place, queries, keys, cum, pair, held)


def two_terms(value):
    high = value.astype(BF16)
    return high, (value - high.astype(F32)).astype(BF16)


def exact(left, right):
    (high, low), (right_high, right_low) = two_terms(left), two_terms(right)
    rows = left.shape[0]
    both = mm(jnp.concatenate([high, low], axis=0), right_high)
    return both[:rows] + (both[rows:] + mm(high, right_low))


def group_kernel(columns, core_ref, mine_ref, other_ref, out_ref):
    def join(first_ref, second_ref):
        for j in range(first_ref.shape[0]):
            joined = exact(second_ref[j][:, :DK], first_ref[j][:, columns])
            out_ref[j] = joined + second_ref[j][:, DK:] if columns.start else joined

    @pl.when(core_ref[2] == 0)
    def _():
        join(mine_ref, other_ref)

    @pl.when(core_ref[2] == 1)
    def _():
        join(other_ref, mine_ref)


def enter_kernel(hops, core_ref, mine_ref, other_ref, former_ref, latter_ref, keep_ref, send_ref):
    early = core_ref[5] < hops

    def through(first_ref, same_ref, out_ref):
        for j in range(first_ref.shape[0]):
            state = jnp.where(early, former_ref[j], latter_ref[j])
            same_ref[j] = state
            out_ref[j] = exact(first_ref[j][:, :DK], state) + first_ref[j][:, DK:]

    @pl.when(core_ref[2] == 0)
    def _():
        through(mine_ref, keep_ref, send_ref)

    @pl.when(core_ref[2] == 1)
    def _():
        through(other_ref, send_ref, keep_ref)


def small_call(kernel, outs, place, *operands):
    part = operands[0].shape[0]
    local = pl.BlockSpec(memory_space=pltpu.VMEM)
    return pl.pallas_call(
        kernel,
        out_shape=[jax.ShapeDtypeStruct((part, DK, DV), F32)] * outs,
        in_specs=[pl.BlockSpec(memory_space=pltpu.SMEM)] + [local] * len(operands),
        out_specs=[local] * outs,
        compiler_params=pltpu.CompilerParams(vmem_limit_bytes=SMALL_VMEM),
    )(place, *operands)


def gated_rows(rows, own, cols, reach_ref, core_ref, gate_ref, gain, state):
    reach = jnp.concatenate([reach_ref[r, own] for r in rows], axis=0)
    core = jnp.concatenate([core_ref[r, own] for r in rows], axis=0)
    gate = jnp.concatenate([gate_ref[r, cols] for r in rows], axis=0).astype(F32)
    core = core + mm(reach, state.astype(BF16))
    normed = core * lax.rsqrt(jnp.mean(core * core, axis=-1, keepdims=True) + 1e-6)
    return (normed * gain * (gate / (1.0 + jnp.exp(-gate)))).astype(BF16)


def part_rows(place_ref, share, offset, size):
    return [pl.ds(pl.multiple_of((i ^ place_ref[3]) * share + offset, 16), size) for i in range(4)]


def early_kernel(
    size, place_ref, reach_ref, core_ref, gate_ref, gain_ref, kept_ref, weight_ref, gated_ref, product_ref
):
    share = gate_ref.shape[0] // 4
    gain = gain_ref[...]
    half = kept_ref.shape[0]
    every = [slice(0, 4 * share)]
    for j in range(half):
        own = slice(j * DV, (j + 1) * DV)
        cols = pl.ds(pl.multiple_of((place_ref[4] + j) * DV, DV), DV)
        gated_ref[:, own] = gated_rows(every, own, cols, reach_ref, core_ref, gate_ref, gain, kept_ref[j])
    first = jnp.concatenate([gated_ref[r, :] for r in part_rows(place_ref, share, 0, size)], axis=0)
    depth = half * DV
    product_ref[...] = mm(first, weight_ref[pl.ds(pl.multiple_of(place_ref[4] * DV, depth), depth), :])


def finish_kernel(offset, place_ref, reach_ref, core_ref, gate_ref, gain_ref, got_ref, weight_ref, early_ref, *refs):
    gated_ref, (send_x_ref, send_y_ref, keep_l_ref, keep_r_ref) = refs[-1], refs[-5:-1]
    product_ref = refs[0] if len(refs) > 5 else None
    size = send_x_ref.shape[1]
    gain = gain_ref[...]
    half = got_ref.shape[0]
    depth = half * DV
    rows = part_rows(place_ref, gate_ref.shape[0] // 4, offset, size)
    for j in range(half):
        own = slice(j * DV, (j + 1) * DV)
        cols = pl.ds(pl.multiple_of((half - place_ref[4] + j) * DV, DV), DV)
        gated_ref[:, own] = gated_rows(rows, own, cols, reach_ref, core_ref, gate_ref, gain, got_ref[j])
    here = pl.ds(pl.multiple_of(place_ref[4] * DV, depth), depth)
    there = pl.ds(pl.multiple_of((half - place_ref[4]) * DV, depth), depth)
    if product_ref is None:
        early = jnp.concatenate([early_ref[r, :] for r in rows], axis=0)
    width = weight_ref.shape[1] // 2
    sums = []
    for cols in (slice(0, width), slice(width, 2 * width)):
        base = mm(early, weight_ref[here, cols]) if product_ref is None else product_ref[:, cols]
        sums.append(base + mm(gated_ref[...], weight_ref[there, cols]))
    left, right = sums
    for i, (l_ref, l_at, r_ref, r_at) in enumerate(
        (
            (keep_l_ref, 0, keep_r_ref, 0),
            (send_x_ref, 0, keep_r_ref, 1),
            (keep_l_ref, 1, send_y_ref, 0),
            (send_x_ref, 1, send_y_ref, 1),
        )
    ):
        l_ref[l_at] = left[i * size : (i + 1) * size]
        r_ref[r_at] = right[i * size : (i + 1) * size]


def begin(size, place, reads, gate, gain, kept, weight):
    tokens = gate.shape[0]
    local = pl.BlockSpec(memory_space=pltpu.VMEM)
    return pl.pallas_call(
        functools.partial(early_kernel, size),
        out_shape=[
            jax.ShapeDtypeStruct((tokens, kept.shape[0] * DV), BF16),
            jax.ShapeDtypeStruct((4 * size, weight.shape[1]), F32),
        ],
        in_specs=[pl.BlockSpec(memory_space=pltpu.SMEM)] + [local] * 6,
        out_specs=[local] * 2,
        compiler_params=pltpu.CompilerParams(vmem_limit_bytes=FINISH_VMEM),
        cost_estimate=pl.CostEstimate(flops=10**9, bytes_accessed=6 * 10**6, transcendentals=tokens * 512),
        name="early",
    )(place, *reads, gate, gain, kept, weight)


def finish(offset, size, place, reads, gate, gain, got, weight, early):
    width = weight.shape[1] // 2
    depth = got.shape[0] * DV
    local = pl.BlockSpec(memory_space=pltpu.VMEM)
    return pl.pallas_call(
        functools.partial(finish_kernel, offset),
        out_shape=[jax.ShapeDtypeStruct((2, size, width), F32)] * 4,
        in_specs=[pl.BlockSpec(memory_space=pltpu.SMEM)] + [local] * (6 + len(early)),
        out_specs=[local] * 4,
        scratch_shapes=[pltpu.VMEM((4 * size, depth), BF16)],
        compiler_params=pltpu.CompilerParams(vmem_limit_bytes=FINISH_VMEM),
        cost_estimate=pl.CostEstimate(
            flops=16 * size * depth * width * 2, bytes_accessed=16 * size * width, transcendentals=8 * size * depth
        ),
        name="finish",
    )(place, *reads, gate, gain, got, weight, *early)


def precise(left, right):
    return jnp.einsum("hij,hjk->hik", left, right, precision=lax.Precision.HIGHEST)


def combine(earlier, later):
    joined = precise(later[..., :DK], earlier)
    return jnp.concatenate([joined[..., :DK], joined[..., DK:] + later[..., DK:]], axis=-1)


def apply_map(pair, state):
    return precise(pair[..., :DK], state) + pair[..., DK:]


def group_hops(pair_map, pair_state, outer, beside=()):
    results, arrivals = [], []
    leaving = pair_state
    for hop in range(outer // 2):
        step = [(i, i + 1) for i in range(hop, outer - 1)] + [(outer - 1, hop)]
        state = lax.ppermute(leaving, "outer", step)
        if hop < len(beside):
            call, place, rest = beside[hop]
            place, _ = lax.optimization_barrier((place, leaving))
            result = call(place, *rest)
            state, result = lax.optimization_barrier((state, result))
            results.append(result)
        arrivals.append(state)
        if hop < outer // 2 - 1:
            if hop:
                state = jnp.where(lax.axis_index("outer") <= hop, arrivals[-2], state)
                arrivals[-1] = state
            leaving = precise(pair_map, state) + pair_state
    return arrivals[-2], arrivals[-1], results


def whole_prefix(mine, theirs, ctx, outer):
    here = lax.axis_index("ctx")
    both = jnp.concatenate([mine, theirs], axis=0)
    blocks = lax.all_gather(both, "ctx")
    identity = jnp.concatenate([jnp.eye(DK, dtype=F32), jnp.zeros((DK, DV), F32)], axis=1)
    start = jnp.broadcast_to(identity, both.shape)

    def hop(k, carry):
        before, through = carry
        through = combine(through, blocks[k])
        return jnp.where(k < here, through, before), through

    before, through = lax.fori_loop(0, ctx, hop, (start, start))
    former, latter, _ = group_hops(through[..., :DK], through[..., DK:], outer)
    entering = jnp.where(lax.axis_index("outer") < outer // 2, former, latter)
    state = apply_map(before, entering)
    half = mine.shape[0]
    return state[:half], state[half:]


def shards(ctx, outer, queries, keys, values, gate, decay, beta, docs, gain, weight):
    heads = decay.shape[0]
    here = lax.axis_index("ctx")
    position = lax.axis_index("outer") * ctx + here
    second = here if ctx == 2 else 0 * here
    group = lax.axis_index("outer")
    place = jnp.stack([1 - second, position, here, lax.axis_index("tp"), second * (heads // 2), group])
    place = place.astype(jnp.int32)
    lengths = lax.broadcast_in_dim(docs, (DOC_ROWS, docs.shape[0]), (1,))
    lengths = jnp.pad(lengths, ((0, 0), (0, decay.shape[1] - docs.shape[0]))).astype(F32)
    rates = jnp.concatenate([decay, beta, lengths], axis=0)
    theirs, mine, pair_t, pair_m, held_t, held_m, cum_t, cum_m = state_maps(place, keys, values, rates)
    if ctx == 2:
        swap = [(0, 1), (1, 0)]
        other = lax.ppermute(theirs, "ctx", swap)
        (group_state,) = small_call(functools.partial(group_kernel, slice(DK, DK + DV)), 1, place, mine, other)
        later, _ = lax.optimization_barrier((place, group_state))
        (group_map,) = small_call(functools.partial(group_kernel, slice(0, DK)), 1, later, mine, other)
        beside = (
            (functools.partial(read_out, 1), place, (queries, keys, cum_m, pair_m, held_m)),
            (functools.partial(read_out, 0), place, (queries, keys, cum_t, pair_t, held_t)),
        )
        former, latter, reads = group_hops(group_map, group_state, outer, beside)
        kept, sent = small_call(functools.partial(enter_kernel, outer // 2), 2, place, mine, other, former, latter)
        got = lax.ppermute(sent, "ctx", swap)
    else:
        kept, got = whole_prefix(mine, theirs, ctx, outer)
        reads = [
            read_out(1, place, queries, keys, cum_m, pair_m, held_m),
            read_out(0, place, queries, keys, cum_t, pair_t, held_t),
        ]
    gain = gain.reshape(1, DV)
    early_place = place
    if ctx == 2:
        early_place, _ = lax.optimization_barrier((place, sent))
    early = begin(PARTS[0], early_place, reads[0], gate, gain, kept, weight)
    along_x = [(i, i ^ 1) for i in range(4)]
    along_y = [(i, i ^ 2) for i in range(4)]
    halves, offset = [], 0
    for size in PARTS:
        send_x, send_y, keep_l, keep_r = finish(offset, size, place, reads[1], gate, gain, got, weight, early[: 1 if offset else 2])
        offset += size
        got_x = lax.ppermute(send_x, "tp", along_x)
        got_y = lax.ppermute(send_y, "tp", along_y)
        halves.append((keep_l, keep_r, got_x, got_y))
    outs = []
    for keep_l, keep_r, got_x, got_y in halves:
        last_l = lax.ppermute(keep_l[1] + got_x[1], "tp", along_y)
        last_r = lax.ppermute(keep_r[1] + got_y[1], "tp", along_x)
        out_l = keep_l[0] + got_x[0] + last_l
        out_r = keep_r[0] + got_y[0] + last_r
        outs.append(jnp.concatenate([out_l, out_r], axis=1).astype(BF16))
    return jnp.concatenate(outs, axis=0)


def solution(mesh):
    ctx, outer = mesh.shape["ctx"], mesh.shape["outer"]
    in_specs = (
        P(("outer", "ctx"), "tp"),
        P(("outer", "ctx"), "tp"),
        P(("outer", "ctx"), "tp"),
        P(("outer", "ctx"), "tp"),
        P("tp", ("outer", "ctx")),
        P("tp", ("outer", "ctx")),
        P(),
        P(),
        P("tp", None),
    )
    out_specs = P(("outer", "ctx", "tp"), None)
    return jax.shard_map(
        functools.partial(shards, ctx, outer), mesh=mesh, in_specs=in_specs, out_specs=out_specs, check_vma=False
    )
```

```python
import functools

import jax
import jax.numpy as jnp
from jax import lax
from jax.experimental import pallas as pl
from jax.experimental.pallas import tpu as pltpu
from jax.sharding import PartitionSpec as P

DK = 128
DV = 128
STRETCH = 64
CHUNK = 2 * STRETCH
F32 = jnp.float32
BF16 = jnp.bfloat16
MIB = 1024 * 1024
MAPS_VMEM = 48 * MIB
READ_VMEM = 12 * MIB
SMALL_VMEM = 4 * MIB
FINISH_VMEM = 16 * MIB
PARTS = (32, 48, 48)
FAR = 1e30


def mm(left, right):
    return jnp.dot(left, right, preferred_element_type=F32)


def unit_rows(raw):
    raw = raw.astype(F32)
    return raw * lax.rsqrt(jnp.sum(raw * raw, axis=-1, keepdims=True) + 1e-6)


def corners(left, right):
    nil = jnp.zeros_like(left)
    return jnp.concatenate(
        [jnp.concatenate([left, nil], axis=1), jnp.concatenate([nil, right], axis=1)], axis=0
    )


def keep_flags(docs_ref, first_stretch, stretches):
    starts, total = [], jnp.int32(0)
    for j in range(docs_ref.shape[0]):
        starts.append(total)
        total = total + docs_ref[j]
    flags = []
    for stretch in range(stretches):
        hit = starts[0] == first_stretch + stretch
        for start in starts[1:]:
            hit = hit | (start == first_stretch + stretch)
        flags.append(jnp.where(hit, 0.0, 1.0).astype(F32))
    return flags


def fade_bias(row, col, k2):
    crossing = (row >= STRETCH) & (col < STRETCH)
    return jnp.where(row >= col, 0.0, -FAR) + jnp.where(crossing, (k2 - 1.0) * FAR, 0.0)


def maps_kernel(
    chunks, key_heads, place_ref, docs_ref, k_hbm, v_hbm, rates_hbm,
    theirs_ref, mine_ref, pair_t_ref, pair_m_ref, held_t_ref, held_m_ref, cum_t_ref, cum_m_ref,
    k_ref, v_ref, rates_ref, sems,
):
    half = key_heads // 2
    loads = [
        pltpu.make_async_copy(src, dst, sems.at[i])
        for i, (src, dst) in enumerate(
            (
                (rates_hbm, rates_ref),
                (k_hbm, k_ref),
                (v_hbm, v_ref),
            )
        )
    ]
    for load in loads:
        load.start()
    row = lax.broadcasted_iota(jnp.int32, (CHUNK, CHUNK), 0)
    col = lax.broadcasted_iota(jnp.int32, (CHUNK, CHUNK), 1)
    upper = (row <= col).astype(F32)
    eye = (row == col).astype(F32)
    below = (row > col).astype(F32)
    apart = row ^ col
    levels = CHUNK.bit_length() - 1
    masks = [((apart >> level) == 1).astype(F32).astype(BF16) for level in range(levels)]
    second = lax.broadcasted_iota(jnp.int32, (1, CHUNK), 1) >= STRETCH
    both_eye = jnp.concatenate([eye, eye], axis=1)
    loads[0].wait()
    heads_all = rates_ref.shape[0] // 2
    keep = keep_flags(docs_ref, place_ref[1] * (2 * chunks), 2 * chunks)
    keeps = [(keep[2 * n], keep[2 * n + 1]) for n in range(chunks)]
    loads[1].wait()

    outs = {}
    for step in range(2):
        side = lax.rem(step + place_ref[0], 2)
        turn = lax.rem(heads_all - 2 * half * side, heads_all)

        def by_chunk(first):
            rolled = pltpu.roll(rates_ref[first : first + heads_all, :], turn, 0)
            return jnp.concatenate(
                [rolled[:, n * CHUNK : (n + 1) * CHUNK] for n in range(chunks)], axis=0
            )

        decay, beta = by_chunk(0), by_chunk(heads_all)
        cum = jnp.dot(decay, upper, precision=lax.Precision.HIGHEST, preferred_element_type=F32)
        cum_ref = (cum_t_ref, cum_m_ref)[step]
        cum_ref[: chunks * heads_all, :] = cum
        for i, flag in enumerate(keep):
            cum_ref[chunks * heads_all + i : chunks * heads_all + i + 1, :] = jnp.full((1, CHUNK), flag, F32)
        grown = jnp.exp(cum)
        cum_col, beta_col = cum.T, beta.T

        pairs = []
        for n in range(chunks):
            rows = slice(n * CHUNK, (n + 1) * CHUNK)
            k1, k2 = keeps[n]
            bias = fade_bias(row, col, k2)
            entry = jnp.where(second, k1 * k2, k1)
            leave = jnp.where(second, 1.0, k2)
            for g in range(half):
                key_cols = pl.ds(pl.multiple_of((side * half + g) * DK, DK), DK)
                k_unit = unit_rows(k_ref[rows, key_cols]).astype(BF16)
                k_turned = k_unit.astype(F32).T
                key_gram = mm(k_unit, k_turned.astype(BF16)) * below
                heads = []
                for e in range(2):
                    at = n * heads_all + 2 * g + e
                    c_row, c_col = cum[at : at + 1, :], cum_col[:, at : at + 1]
                    b_row = beta[at : at + 1, :]
                    fade = jnp.exp((c_col - c_row) + bias)
                    last = c_row[:, CHUNK - 1 : CHUNK]
                    heads.append(
                        dict(
                            noise=(key_gram * fade * beta_col[:, at : at + 1]).astype(BF16),
                            b_row=b_row,
                            be_row=b_row * grown[at : at + 1, :] * entry,
                            k_out=(k_turned * (jnp.exp(last - c_row) * leave)).astype(BF16),
                            through=jnp.exp(last) * (k1 * k2),
                        )
                    )
                pairs.append((n, g, k_unit, heads))

        inverses = [
            both_eye - jnp.concatenate([h["noise"] * masks[0] for h in heads], axis=1).astype(F32)
            for _, _, _, heads in pairs
        ]
        for level in range(1, levels):
            held = [t.astype(BF16) for t in inverses]
            part = [
                mm(t, corners(heads[0]["noise"] * masks[level], heads[1]["noise"] * masks[level])).astype(BF16)
                for t, (_, _, _, heads) in zip(held, pairs)
            ]
            inverses = [
                t - mm(p, corners(b[:, :CHUNK], b[:, CHUNK:])) for t, p, b in zip(inverses, part, held)
            ]

        if step == 0:
            loads[2].wait()
        pair_ref = (pair_t_ref, pair_m_ref)[step]
        for (n, g, k_unit, heads), t in zip(pairs, inverses):
            rows = slice(n * CHUNK, (n + 1) * CHUNK)
            values = v_ref[rows, pl.ds(pl.multiple_of((side * half + g) * 2 * DV, 2 * DV), 2 * DV)]
            b_rows = jnp.concatenate([h["b_row"] for h in heads], axis=1)
            wy_values = mm((t * b_rows).astype(BF16), corners(values[:, :DV], values[:, DV:])).astype(BF16)
            weighted = jnp.concatenate(
                [t[:, e * CHUNK : (e + 1) * CHUNK] * heads[e]["be_row"] for e in range(2)], axis=0
            )
            wy_keys = mm(weighted.astype(BF16), k_unit).astype(BF16)
            for e in range(2):
                pair = jnp.concatenate(
                    [wy_keys[e * CHUNK : (e + 1) * CHUNK], wy_values[:, e * DV : (e + 1) * DV]], axis=1
                )
                pair_ref[2 * g + e, rows, :] = pair
                outs[step, n, 2 * g + e] = (mm(heads[e]["k_out"], pair), heads[e]["through"])

    carried = {}
    for n in range(chunks):
        for step in range(2):
            for j in range(2 * half):
                moved, through = outs[step, n, j]
                if n == 0:
                    carried[step, j] = jnp.concatenate([eye * through - moved[:, :DK], moved[:, DK:]], axis=1)
                    continue
                held = carried[step, j].astype(BF16)
                (held_t_ref, held_m_ref)[step][j, n - 1] = held
                after = carried[step, j] * through - mm(moved[:, :DK].astype(BF16), held)
                carried[step, j] = jnp.concatenate([after[:, :DK], after[:, DK:] + moved[:, DK:]], axis=1)
    for j in range(2 * half):
        theirs_ref[j] = carried[0, j]
        mine_ref[j] = carried[1, j]


def state_maps(place, docs, keys, values, rates):
    tokens, key_width = keys.shape
    key_heads = key_width // DK
    heads = rates.shape[0] // 2
    chunks = tokens // CHUNK
    part = heads // 2
    local = pl.BlockSpec(memory_space=pltpu.VMEM)
    remote = pl.BlockSpec(memory_space=pltpu.HBM)
    return pl.pallas_call(
        functools.partial(maps_kernel, chunks, key_heads),
        out_shape=[jax.ShapeDtypeStruct((part, DK, DK + DV), F32)] * 2
        + [jax.ShapeDtypeStruct((part, tokens, DK + DV), BF16)] * 2
        + [jax.ShapeDtypeStruct((part, chunks - 1, DK, DK + DV), BF16)] * 2
        + [jax.ShapeDtypeStruct((chunks * (heads + 2), CHUNK), F32)] * 2,
        in_specs=[pl.BlockSpec(memory_space=pltpu.SMEM)] * 2 + [remote] * 3,
        out_specs=[local] * 8,
        scratch_shapes=[
            pltpu.VMEM(keys.shape, keys.dtype),
            pltpu.VMEM(values.shape, values.dtype),
            pltpu.VMEM(rates.shape, rates.dtype),
            pltpu.SemaphoreType.DMA((3,)),
        ],
        compiler_params=pltpu.CompilerParams(vmem_limit_bytes=MAPS_VMEM),
        name="state_maps",
    )(place, docs, keys, values, rates)


def read_kernel(
    step, chunks, key_heads, place_ref, q_ref, k_ref, cum_ref, pair_ref, held_ref, reach_ref, core_ref
):
    half = key_heads // 2
    side = lax.rem(step + place_ref[0], 2)
    heads_all = 4 * half
    row = lax.broadcasted_iota(jnp.int32, (CHUNK, CHUNK), 0)
    col = lax.broadcasted_iota(jnp.int32, (CHUNK, CHUNK), 1)
    second_col = lax.broadcasted_iota(jnp.int32, (CHUNK, 1), 0) >= STRETCH
    keep = cum_ref[chunks * heads_all :, :]
    keeps = [(keep[2 * n : 2 * n + 1, 0:1], keep[2 * n + 1 : 2 * n + 2, 0:1]) for n in range(chunks)]
    cum = cum_ref[: chunks * heads_all, :]
    cum_col = cum.T
    grown_col = jnp.exp(cum_col)
    for n in range(chunks):
        rows = slice(n * CHUNK, (n + 1) * CHUNK)
        k1, k2 = keeps[n]
        bias = fade_bias(row, col, k2)
        entry_col = jnp.where(second_col, k1 * k2, k1)
        for g in range(half):
            key_cols = pl.ds(pl.multiple_of((side * half + g) * DK, DK), DK)
            k_unit = unit_rows(k_ref[rows, key_cols]).astype(BF16)
            q_unit = unit_rows(q_ref[rows, key_cols]).astype(BF16)
            query_gram = mm(q_unit, k_unit.astype(F32).T.astype(BF16))
            for e in range(2):
                j = 2 * g + e
                at = n * heads_all + j
                cols = slice(j * DV, (j + 1) * DV)
                fade = jnp.exp((cum_col[:, at : at + 1] - cum[at : at + 1, :]) + bias)
                seen = mm((query_gram * fade).astype(BF16), pair_ref[j, rows, :])
                q_in = q_unit.astype(F32) * (grown_col[:, at : at + 1] * entry_col)
                q_eff = (q_in - seen[:, :DK]).astype(BF16)
                if n == 0:
                    reach_ref[rows, cols] = q_eff
                    core_ref[rows, cols] = seen[:, DK:]
                else:
                    read = mm(q_eff, held_ref[j, n - 1])
                    reach_ref[rows, cols] = read[:, :DK].astype(BF16)
                    core_ref[rows, cols] = read[:, DK:] + seen[:, DK:]


def read_out(step, place, queries, keys, cum, pair, held):
    tokens, key_width = queries.shape
    key_heads = key_width // DK
    chunks = tokens // CHUNK
    local = pl.BlockSpec(memory_space=pltpu.VMEM)
    scalar = pl.BlockSpec(memory_space=pltpu.SMEM)
    width = pair.shape[0] * DV
    return pl.pallas_call(
        functools.partial(read_kernel, step, chunks, key_heads),
        out_shape=[
            jax.ShapeDtypeStruct((tokens, width), BF16),
            jax.ShapeDtypeStruct((tokens, width), F32),
        ],
        in_specs=[scalar] + [local] * 5,
        out_specs=[local] * 2,
        compiler_params=pltpu.CompilerParams(vmem_limit_bytes=READ_VMEM),
        cost_estimate=pl.CostEstimate(flops=2 * 10**9, bytes_accessed=6 * 10**6, transcendentals=10**6),
        name="read_out",
    )(place, queries, keys, cum, pair, held)


def two_terms(value):
    high = value.astype(BF16)
    return high, (value - high.astype(F32)).astype(BF16)


def exact(left, right):
    (high, low), (right_high, right_low) = two_terms(left), two_terms(right)
    rows = left.shape[0]
    both = mm(jnp.concatenate([high, low], axis=0), right_high)
    return both[:rows] + (both[rows:] + mm(high, right_low))


def group_kernel(columns, core_ref, mine_ref, other_ref, out_ref):
    def join(first_ref, second_ref):
        for j in range(first_ref.shape[0]):
            joined = exact(second_ref[j][:, :DK], first_ref[j][:, columns])
            out_ref[j] = joined + second_ref[j][:, DK:] if columns.start else joined

    @pl.when(core_ref[2] == 0)
    def _():
        join(mine_ref, other_ref)

    @pl.when(core_ref[2] == 1)
    def _():
        join(other_ref, mine_ref)


def enter_kernel(hops, core_ref, mine_ref, other_ref, former_ref, latter_ref, keep_ref, send_ref):
    early = core_ref[5] < hops

    def through(first_ref, same_ref, out_ref):
        for j in range(first_ref.shape[0]):
            state = jnp.where(early, former_ref[j], latter_ref[j])
            same_ref[j] = state
            out_ref[j] = exact(first_ref[j][:, :DK], state) + first_ref[j][:, DK:]

    @pl.when(core_ref[2] == 0)
    def _():
        through(mine_ref, keep_ref, send_ref)

    @pl.when(core_ref[2] == 1)
    def _():
        through(other_ref, send_ref, keep_ref)


def small_call(kernel, outs, place, *operands):
    part = operands[0].shape[0]
    local = pl.BlockSpec(memory_space=pltpu.VMEM)
    return pl.pallas_call(
        kernel,
        out_shape=[jax.ShapeDtypeStruct((part, DK, DV), F32)] * outs,
        in_specs=[pl.BlockSpec(memory_space=pltpu.SMEM)] + [local] * len(operands),
        out_specs=[local] * outs,
        compiler_params=pltpu.CompilerParams(vmem_limit_bytes=SMALL_VMEM),
    )(place, *operands)


def gated_rows(rows, own, cols, reach_ref, core_ref, gate_ref, gain, state):
    reach = jnp.concatenate([reach_ref[r, own] for r in rows], axis=0)
    core = jnp.concatenate([core_ref[r, own] for r in rows], axis=0)
    gate = jnp.concatenate([gate_ref[r, cols] for r in rows], axis=0).astype(F32)
    core = core + mm(reach, state.astype(BF16))
    normed = core * lax.rsqrt(jnp.mean(core * core, axis=-1, keepdims=True) + 1e-6)
    return (normed * gain * (gate / (1.0 + jnp.exp(-gate)))).astype(BF16)


def part_rows(place_ref, share, offset, size):
    return [pl.ds(pl.multiple_of((i ^ place_ref[3]) * share + offset, 16), size) for i in range(4)]


def early_kernel(
    size, place_ref, reach_ref, core_ref, gate_ref, gain_ref, kept_ref, weight_ref, gated_ref, product_ref
):
    share = gate_ref.shape[0] // 4
    gain = gain_ref[...]
    half = kept_ref.shape[0]
    every = [slice(0, 4 * share)]
    for j in range(half):
        own = slice(j * DV, (j + 1) * DV)
        cols = pl.ds(pl.multiple_of((place_ref[4] + j) * DV, DV), DV)
        gated_ref[:, own] = gated_rows(every, own, cols, reach_ref, core_ref, gate_ref, gain, kept_ref[j])
    first = jnp.concatenate([gated_ref[r, :] for r in part_rows(place_ref, share, 0, size)], axis=0)
    depth = half * DV
    product_ref[...] = mm(first, weight_ref[pl.ds(pl.multiple_of(place_ref[4] * DV, depth), depth), :])


def finish_kernel(offset, place_ref, reach_ref, core_ref, gate_ref, gain_ref, got_ref, weight_ref, early_ref, *refs):
    gated_ref, (send_x_ref, send_y_ref, keep_l_ref, keep_r_ref) = refs[-1], refs[-5:-1]
    product_ref = refs[0] if len(refs) > 5 else None
    size = send_x_ref.shape[1]
    gain = gain_ref[...]
    half = got_ref.shape[0]
    depth = half * DV
    rows = part_rows(place_ref, gate_ref.shape[0] // 4, offset, size)
    for j in range(half):
        own = slice(j * DV, (j + 1) * DV)
        cols = pl.ds(pl.multiple_of((half - place_ref[4] + j) * DV, DV), DV)
        gated_ref[:, own] = gated_rows(rows, own, cols, reach_ref, core_ref, gate_ref, gain, got_ref[j])
    here = pl.ds(pl.multiple_of(place_ref[4] * DV, depth), depth)
    there = pl.ds(pl.multiple_of((half - place_ref[4]) * DV, depth), depth)
    if product_ref is None:
        early = jnp.concatenate([early_ref[r, :] for r in rows], axis=0)
    width = weight_ref.shape[1] // 2
    sums = []
    for cols in (slice(0, width), slice(width, 2 * width)):
        base = mm(early, weight_ref[here, cols]) if product_ref is None else product_ref[:, cols]
        sums.append(base + mm(gated_ref[...], weight_ref[there, cols]))
    left, right = sums
    for i, (l_ref, l_at, r_ref, r_at) in enumerate(
        (
            (keep_l_ref, 0, keep_r_ref, 0),
            (send_x_ref, 0, keep_r_ref, 1),
            (keep_l_ref, 1, send_y_ref, 0),
            (send_x_ref, 1, send_y_ref, 1),
        )
    ):
        l_ref[l_at] = left[i * size : (i + 1) * size]
        r_ref[r_at] = right[i * size : (i + 1) * size]


def begin(size, place, reads, gate, gain, kept, weight):
    tokens = gate.shape[0]
    local = pl.BlockSpec(memory_space=pltpu.VMEM)
    return pl.pallas_call(
        functools.partial(early_kernel, size),
        out_shape=[
            jax.ShapeDtypeStruct((tokens, kept.shape[0] * DV), BF16),
            jax.ShapeDtypeStruct((4 * size, weight.shape[1]), F32),
        ],
        in_specs=[pl.BlockSpec(memory_space=pltpu.SMEM)] + [local] * 6,
        out_specs=[local] * 2,
        compiler_params=pltpu.CompilerParams(vmem_limit_bytes=FINISH_VMEM),
        cost_estimate=pl.CostEstimate(flops=10**9, bytes_accessed=6 * 10**6, transcendentals=tokens * 512),
        name="early",
    )(place, *reads, gate, gain, kept, weight)


def finish(offset, size, place, reads, gate, gain, got, weight, early):
    width = weight.shape[1] // 2
    depth = got.shape[0] * DV
    local = pl.BlockSpec(memory_space=pltpu.VMEM)
    return pl.pallas_call(
        functools.partial(finish_kernel, offset),
        out_shape=[jax.ShapeDtypeStruct((2, size, width), F32)] * 4,
        in_specs=[pl.BlockSpec(memory_space=pltpu.SMEM)] + [local] * (6 + len(early)),
        out_specs=[local] * 4,
        scratch_shapes=[pltpu.VMEM((4 * size, depth), BF16)],
        compiler_params=pltpu.CompilerParams(vmem_limit_bytes=FINISH_VMEM),
        cost_estimate=pl.CostEstimate(
            flops=16 * size * depth * width * 2, bytes_accessed=16 * size * width, transcendentals=8 * size * depth
        ),
        name="finish",
    )(place, *reads, gate, gain, got, weight, *early)


def precise(left, right):
    return jnp.einsum("hij,hjk->hik", left, right, precision=lax.Precision.HIGHEST)


def combine(earlier, later):
    joined = precise(later[..., :DK], earlier)
    return jnp.concatenate([joined[..., :DK], joined[..., DK:] + later[..., DK:]], axis=-1)


def apply_map(pair, state):
    return precise(pair[..., :DK], state) + pair[..., DK:]


def group_hops(pair_map, pair_state, outer, beside=()):
    results, arrivals = [], []
    leaving = pair_state
    for hop in range(outer // 2):
        step = [(i, i + 1) for i in range(hop, outer - 1)] + [(outer - 1, hop)]
        state = lax.ppermute(leaving, "outer", step)
        if hop < len(beside):
            call, place, rest = beside[hop]
            place, _ = lax.optimization_barrier((place, leaving))
            result = call(place, *rest)
            state, result = lax.optimization_barrier((state, result))
            results.append(result)
        arrivals.append(state)
        if hop < outer // 2 - 1:
            if hop:
                state = jnp.where(lax.axis_index("outer") <= hop, arrivals[-2], state)
                arrivals[-1] = state
            leaving = precise(pair_map, state) + pair_state
    return arrivals[-2], arrivals[-1], results


def whole_prefix(mine, theirs, ctx, outer):
    here = lax.axis_index("ctx")
    both = jnp.concatenate([mine, theirs], axis=0)
    blocks = lax.all_gather(both, "ctx")
    identity = jnp.concatenate([jnp.eye(DK, dtype=F32), jnp.zeros((DK, DV), F32)], axis=1)
    start = jnp.broadcast_to(identity, both.shape)

    def hop(k, carry):
        before, through = carry
        through = combine(through, blocks[k])
        return jnp.where(k < here, through, before), through

    before, through = lax.fori_loop(0, ctx, hop, (start, start))
    former, latter, _ = group_hops(through[..., :DK], through[..., DK:], outer)
    entering = jnp.where(lax.axis_index("outer") < outer // 2, former, latter)
    state = apply_map(before, entering)
    half = mine.shape[0]
    return state[:half], state[half:]


def shards(ctx, outer, queries, keys, values, gate, decay, beta, docs, gain, weight):
    heads = decay.shape[0]
    here = lax.axis_index("ctx")
    position = lax.axis_index("outer") * ctx + here
    second = here if ctx == 2 else 0 * here
    group = lax.axis_index("outer")
    place = jnp.stack([1 - second, position, here, lax.axis_index("tp"), second * (heads // 2), group])
    place = place.astype(jnp.int32)
    rates = jnp.concatenate([decay, beta], axis=0)
    theirs, mine, pair_t, pair_m, held_t, held_m, cum_t, cum_m = state_maps(place, docs, keys, values, rates)
    if ctx == 2:
        swap = [(0, 1), (1, 0)]
        other = lax.ppermute(theirs, "ctx", swap)
        (group_state,) = small_call(functools.partial(group_kernel, slice(DK, DK + DV)), 1, place, mine, other)
        later, _ = lax.optimization_barrier((place, group_state))
        (group_map,) = small_call(functools.partial(group_kernel, slice(0, DK)), 1, later, mine, other)
        beside = (
            (functools.partial(read_out, 1), place, (queries, keys, cum_m, pair_m, held_m)),
            (functools.partial(read_out, 0), place, (queries, keys, cum_t, pair_t, held_t)),
        )
        former, latter, reads = group_hops(group_map, group_state, outer, beside)
        kept, sent = small_call(functools.partial(enter_kernel, outer // 2), 2, place, mine, other, former, latter)
        got = lax.ppermute(sent, "ctx", swap)
    else:
        kept, got = whole_prefix(mine, theirs, ctx, outer)
        reads = [
            read_out(1, place, queries, keys, cum_m, pair_m, held_m),
            read_out(0, place, queries, keys, cum_t, pair_t, held_t),
        ]
    gain = gain.reshape(1, DV)
    early_place = place
    if ctx == 2:
        early_place, _ = lax.optimization_barrier((place, sent))
    early = begin(PARTS[0], early_place, reads[0], gate, gain, kept, weight)
    along_x = [(i, i ^ 1) for i in range(4)]
    along_y = [(i, i ^ 2) for i in range(4)]
    halves, offset = [], 0
    for size in PARTS:
        send_x, send_y, keep_l, keep_r = finish(offset, size, place, reads[1], gate, gain, got, weight, early[: 1 if offset else 2])
        offset += size
        got_x = lax.ppermute(send_x, "tp", along_x)
        got_y = lax.ppermute(send_y, "tp", along_y)
        halves.append((keep_l, keep_r, got_x, got_y))
    outs = []
    for keep_l, keep_r, got_x, got_y in halves:
        last_l = lax.ppermute(keep_l[1] + got_x[1], "tp", along_y)
        last_r = lax.ppermute(keep_r[1] + got_y[1], "tp", along_x)
        out_l = keep_l[0] + got_x[0] + last_l
        out_r = keep_r[0] + got_y[0] + last_r
        outs.append(jnp.concatenate([out_l, out_r], axis=1).astype(BF16))
    return jnp.concatenate(outs, axis=0)


def solution(mesh):
    ctx, outer = mesh.shape["ctx"], mesh.shape["outer"]
    in_specs = (
        P(("outer", "ctx"), "tp"),
        P(("outer", "ctx"), "tp"),
        P(("outer", "ctx"), "tp"),
        P(("outer", "ctx"), "tp"),
        P("tp", ("outer", "ctx")),
        P("tp", ("outer", "ctx")),
        P(),
        P(),
        P("tp", None),
    )
    out_specs = P(("outer", "ctx", "tp"), None)
    return jax.shard_map(
        functools.partial(shards, ctx, outer), mesh=mesh, in_specs=in_specs, out_specs=out_specs, check_vma=False
    )
```

```python
import functools

import jax
import jax.numpy as jnp
from jax import lax
from jax.experimental import pallas as pl
from jax.experimental.pallas import tpu as pltpu
from jax.sharding import PartitionSpec as P

DK = 128
DV = 128
STRETCH = 64
CHUNK = 2 * STRETCH
F32 = jnp.float32
BF16 = jnp.bfloat16
MIB = 1024 * 1024
MAPS_VMEM = 48 * MIB
READ_VMEM = 12 * MIB
SMALL_VMEM = 4 * MIB
FINISH_VMEM = 16 * MIB
PARTS = (32, 48, 48)
DOC_ROWS = 8
FAR = 1e30


def mm(left, right):
    return jnp.dot(left, right, preferred_element_type=F32)


def unit_rows(raw):
    raw = raw.astype(F32)
    return raw * lax.rsqrt(jnp.sum(raw * raw, axis=-1, keepdims=True) + 1e-6)


def corners(left, right):
    nil = jnp.zeros_like(left)
    return jnp.concatenate(
        [jnp.concatenate([left, nil], axis=1), jnp.concatenate([nil, right], axis=1)], axis=0
    )


def keep_flags(docs, first_stretch, stretches):
    before = lax.broadcasted_iota(jnp.int32, (CHUNK, CHUNK), 0) < lax.broadcasted_iota(jnp.int32, (CHUNK, CHUNK), 1)
    starts = mm(docs.astype(BF16), before.astype(F32).astype(BF16))[0:1, :]
    ids = (lax.broadcasted_iota(jnp.int32, (stretches, CHUNK), 0) + first_stretch).astype(F32)
    return 1.0 - jnp.max(jnp.where(ids == starts, 1.0, 0.0), axis=1, keepdims=True)


def fade_bias(row, col, k2):
    crossing = (row >= STRETCH) & (col < STRETCH)
    return jnp.where(row >= col, 0.0, -FAR) + jnp.where(crossing, (k2 - 1.0) * FAR, 0.0)


def maps_kernel(
    chunks, key_heads, place_ref, k_hbm, v_hbm, rates_hbm,
    theirs_ref, mine_ref, pair_t_ref, pair_m_ref, held_t_ref, held_m_ref, cum_t_ref, cum_m_ref,
    k_ref, v_ref, rates_ref, sems,
):
    half = key_heads // 2
    loads = [
        pltpu.make_async_copy(src, dst, sems.at[i])
        for i, (src, dst) in enumerate(
            (
                (rates_hbm, rates_ref),
                (k_hbm, k_ref),
                (v_hbm, v_ref),
            )
        )
    ]
    for load in loads:
        load.start()
    row = lax.broadcasted_iota(jnp.int32, (CHUNK, CHUNK), 0)
    col = lax.broadcasted_iota(jnp.int32, (CHUNK, CHUNK), 1)
    upper = (row <= col).astype(F32)
    eye = (row == col).astype(F32)
    below = (row > col).astype(F32)
    apart = row ^ col
    levels = CHUNK.bit_length() - 1
    masks = [((apart >> level) == 1).astype(F32).astype(BF16) for level in range(levels)]
    second = lax.broadcasted_iota(jnp.int32, (1, CHUNK), 1) >= STRETCH
    both_eye = jnp.concatenate([eye, eye], axis=1)
    loads[0].wait()
    heads_all = (rates_ref.shape[0] - DOC_ROWS) // 2
    keep = keep_flags(rates_ref[2 * heads_all :, :CHUNK], place_ref[1] * (2 * chunks), 2 * chunks)
    keeps = [(keep[2 * n : 2 * n + 1], keep[2 * n + 1 : 2 * n + 2]) for n in range(chunks)]
    loads[1].wait()

    outs = {}
    for step in range(2):
        side = lax.rem(step + place_ref[0], 2)
        turn = lax.rem(heads_all - 2 * half * side, heads_all)

        def by_chunk(first):
            rolled = pltpu.roll(rates_ref[first : first + heads_all, :], turn, 0)
            return jnp.concatenate(
                [rolled[:, n * CHUNK : (n + 1) * CHUNK] for n in range(chunks)], axis=0
            )

        decay, beta = by_chunk(0), by_chunk(heads_all)
        cum = jnp.dot(decay, upper, precision=lax.Precision.HIGHEST, preferred_element_type=F32)
        cum_ref = (cum_t_ref, cum_m_ref)[step]
        cum_ref[: chunks * heads_all, :] = cum
        cum_ref[chunks * heads_all :, :] = jnp.broadcast_to(keep, (2 * chunks, CHUNK))
        grown = jnp.exp(cum)
        cum_col, beta_col = cum.T, beta.T

        pairs = []
        for n in range(chunks):
            rows = slice(n * CHUNK, (n + 1) * CHUNK)
            k1, k2 = keeps[n]
            bias = fade_bias(row, col, k2)
            entry = jnp.where(second, k1 * k2, k1)
            leave = jnp.where(second, 1.0, k2)
            for g in range(half):
                key_cols = pl.ds(pl.multiple_of((side * half + g) * DK, DK), DK)
                k_unit = unit_rows(k_ref[rows, key_cols]).astype(BF16)
                k_turned = k_unit.astype(F32).T
                key_gram = mm(k_unit, k_turned.astype(BF16)) * below
                heads = []
                for e in range(2):
                    at = n * heads_all + 2 * g + e
                    c_row, c_col = cum[at : at + 1, :], cum_col[:, at : at + 1]
                    b_row = beta[at : at + 1, :]
                    fade = jnp.exp((c_col - c_row) + bias)
                    last = c_row[:, CHUNK - 1 : CHUNK]
                    heads.append(
                        dict(
                            noise=(key_gram * fade * beta_col[:, at : at + 1]).astype(BF16),
                            b_row=b_row,
                            be_row=b_row * grown[at : at + 1, :] * entry,
                            k_out=(k_turned * (jnp.exp(last - c_row) * leave)).astype(BF16),
                            through=jnp.exp(last) * (k1 * k2),
                        )
                    )
                pairs.append((n, g, k_unit, heads))

        inverses = [
            both_eye - jnp.concatenate([h["noise"] * masks[0] for h in heads], axis=1).astype(F32)
            for _, _, _, heads in pairs
        ]
        for level in range(1, levels):
            held = [t.astype(BF16) for t in inverses]
            part = [
                mm(t, corners(heads[0]["noise"] * masks[level], heads[1]["noise"] * masks[level])).astype(BF16)
                for t, (_, _, _, heads) in zip(held, pairs)
            ]
            inverses = [
                t - mm(p, corners(b[:, :CHUNK], b[:, CHUNK:])) for t, p, b in zip(inverses, part, held)
            ]

        if step == 0:
            loads[2].wait()
        pair_ref = (pair_t_ref, pair_m_ref)[step]
        for (n, g, k_unit, heads), t in zip(pairs, inverses):
            rows = slice(n * CHUNK, (n + 1) * CHUNK)
            values = v_ref[rows, pl.ds(pl.multiple_of((side * half + g) * 2 * DV, 2 * DV), 2 * DV)]
            b_rows = jnp.concatenate([h["b_row"] for h in heads], axis=1)
            wy_values = mm((t * b_rows).astype(BF16), corners(values[:, :DV], values[:, DV:])).astype(BF16)
            weighted = jnp.concatenate(
                [t[:, e * CHUNK : (e + 1) * CHUNK] * heads[e]["be_row"] for e in range(2)], axis=0
            )
            wy_keys = mm(weighted.astype(BF16), k_unit).astype(BF16)
            for e in range(2):
                pair = jnp.concatenate(
                    [wy_keys[e * CHUNK : (e + 1) * CHUNK], wy_values[:, e * DV : (e + 1) * DV]], axis=1
                )
                pair_ref[2 * g + e, rows, :] = pair
                outs[step, n, 2 * g + e] = (mm(heads[e]["k_out"], pair), heads[e]["through"])

    carried = {}
    for n in range(chunks):
        for step in range(2):
            for j in range(2 * half):
                moved, through = outs[step, n, j]
                if n == 0:
                    carried[step, j] = jnp.concatenate([eye * through - moved[:, :DK], moved[:, DK:]], axis=1)
                    continue
                held = carried[step, j].astype(BF16)
                (held_t_ref, held_m_ref)[step][j, n - 1] = held
                after = carried[step, j] * through - mm(moved[:, :DK].astype(BF16), held)
                carried[step, j] = jnp.concatenate([after[:, :DK], after[:, DK:] + moved[:, DK:]], axis=1)
    for j in range(2 * half):
        theirs_ref[j] = carried[0, j]
        mine_ref[j] = carried[1, j]


def state_maps(place, keys, values, rates):
    tokens, key_width = keys.shape
    key_heads = key_width // DK
    heads = (rates.shape[0] - DOC_ROWS) // 2
    chunks = tokens // CHUNK
    part = heads // 2
    local = pl.BlockSpec(memory_space=pltpu.VMEM)
    remote = pl.BlockSpec(memory_space=pltpu.HBM)
    return pl.pallas_call(
        functools.partial(maps_kernel, chunks, key_heads),
        out_shape=[jax.ShapeDtypeStruct((part, DK, DK + DV), F32)] * 2
        + [jax.ShapeDtypeStruct((part, tokens, DK + DV), BF16)] * 2
        + [jax.ShapeDtypeStruct((part, chunks - 1, DK, DK + DV), BF16)] * 2
        + [jax.ShapeDtypeStruct((chunks * (heads + 2), CHUNK), F32)] * 2,
        in_specs=[pl.BlockSpec(memory_space=pltpu.SMEM)] + [remote] * 3,
        out_specs=[local] * 8,
        scratch_shapes=[
            pltpu.VMEM(keys.shape, keys.dtype),
            pltpu.VMEM(values.shape, values.dtype),
            pltpu.VMEM(rates.shape, rates.dtype),
            pltpu.SemaphoreType.DMA((3,)),
        ],
        compiler_params=pltpu.CompilerParams(vmem_limit_bytes=MAPS_VMEM),
        name="state_maps",
    )(place, keys, values, rates)


def read_kernel(
    step, chunks, key_heads, place_ref, q_ref, k_ref, cum_ref, pair_ref, held_ref, reach_ref, core_ref
):
    half = key_heads // 2
    side = lax.rem(step + place_ref[0], 2)
    heads_all = 4 * half
    row = lax.broadcasted_iota(jnp.int32, (CHUNK, CHUNK), 0)
    col = lax.broadcasted_iota(jnp.int32, (CHUNK, CHUNK), 1)
    second_col = lax.broadcasted_iota(jnp.int32, (CHUNK, 1), 0) >= STRETCH
    keep = cum_ref[chunks * heads_all :, :]
    keeps = [(keep[2 * n : 2 * n + 1, 0:1], keep[2 * n + 1 : 2 * n + 2, 0:1]) for n in range(chunks)]
    cum = cum_ref[: chunks * heads_all, :]
    cum_col = cum.T
    grown_col = jnp.exp(cum_col)
    for n in range(chunks):
        rows = slice(n * CHUNK, (n + 1) * CHUNK)
        k1, k2 = keeps[n]
        bias = fade_bias(row, col, k2)
        entry_col = jnp.where(second_col, k1 * k2, k1)
        for g in range(half):
            key_cols = pl.ds(pl.multiple_of((side * half + g) * DK, DK), DK)
            k_unit = unit_rows(k_ref[rows, key_cols]).astype(BF16)
            q_unit = unit_rows(q_ref[rows, key_cols]).astype(BF16)
            query_gram = mm(q_unit, k_unit.astype(F32).T.astype(BF16))
            for e in range(2):
                j = 2 * g + e
                at = n * heads_all + j
                cols = slice(j * DV, (j + 1) * DV)
                fade = jnp.exp((cum_col[:, at : at + 1] - cum[at : at + 1, :]) + bias)
                seen = mm((query_gram * fade).astype(BF16), pair_ref[j, rows, :])
                q_in = q_unit.astype(F32) * (grown_col[:, at : at + 1] * entry_col)
                q_eff = (q_in - seen[:, :DK]).astype(BF16)
                if n == 0:
                    reach_ref[rows, cols] = q_eff
                    core_ref[rows, cols] = seen[:, DK:]
                else:
                    read = mm(q_eff, held_ref[j, n - 1])
                    reach_ref[rows, cols] = read[:, :DK].astype(BF16)
                    core_ref[rows, cols] = read[:, DK:] + seen[:, DK:]


def read_out(step, place, queries, keys, cum, pair, held):
    tokens, key_width = queries.shape
    key_heads = key_width // DK
    chunks = tokens // CHUNK
    local = pl.BlockSpec(memory_space=pltpu.VMEM)
    scalar = pl.BlockSpec(memory_space=pltpu.SMEM)
    width = pair.shape[0] * DV
    return pl.pallas_call(
        functools.partial(read_kernel, step, chunks, key_heads),
        out_shape=[
            jax.ShapeDtypeStruct((tokens, width), BF16),
            jax.ShapeDtypeStruct((tokens, width), F32),
        ],
        in_specs=[scalar] + [local] * 5,
        out_specs=[local] * 2,
        compiler_params=pltpu.CompilerParams(vmem_limit_bytes=READ_VMEM),
        cost_estimate=pl.CostEstimate(flops=2 * 10**9, bytes_accessed=6 * 10**6, transcendentals=10**6),
        name="read_out",
    )(place, queries, keys, cum, pair, held)


def two_terms(value):
    high = value.astype(BF16)
    return high, (value - high.astype(F32)).astype(BF16)


def exact(left, right):
    (high, low), (right_high, right_low) = two_terms(left), two_terms(right)
    rows = left.shape[0]
    both = mm(jnp.concatenate([high, low], axis=0), right_high)
    return both[:rows] + (both[rows:] + mm(high, right_low))


def group_kernel(columns, core_ref, mine_ref, other_ref, out_ref):
    def join(first_ref, second_ref):
        for j in range(first_ref.shape[0]):
            joined = exact(second_ref[j][:, :DK], first_ref[j][:, columns])
            out_ref[j] = joined + second_ref[j][:, DK:] if columns.start else joined

    @pl.when(core_ref[2] == 0)
    def _():
        join(mine_ref, other_ref)

    @pl.when(core_ref[2] == 1)
    def _():
        join(other_ref, mine_ref)


def enter_kernel(hops, core_ref, mine_ref, other_ref, former_ref, latter_ref, keep_ref, send_ref):
    early = core_ref[5] < hops

    def through(first_ref, same_ref, out_ref):
        for j in range(first_ref.shape[0]):
            state = jnp.where(early, former_ref[j], latter_ref[j])
            same_ref[j] = state
            out_ref[j] = exact(first_ref[j][:, :DK], state) + first_ref[j][:, DK:]

    @pl.when(core_ref[2] == 0)
    def _():
        through(mine_ref, keep_ref, send_ref)

    @pl.when(core_ref[2] == 1)
    def _():
        through(other_ref, send_ref, keep_ref)


def small_call(kernel, outs, place, *operands):
    part = operands[0].shape[0]
    local = pl.BlockSpec(memory_space=pltpu.VMEM)
    return pl.pallas_call(
        kernel,
        out_shape=[jax.ShapeDtypeStruct((part, DK, DV), F32)] * outs,
        in_specs=[pl.BlockSpec(memory_space=pltpu.SMEM)] + [local] * len(operands),
        out_specs=[local] * outs,
        compiler_params=pltpu.CompilerParams(vmem_limit_bytes=SMALL_VMEM),
    )(place, *operands)


def gated_rows(rows, own, cols, reach_ref, core_ref, gate_ref, gain, state):
    reach = jnp.concatenate([reach_ref[r, own] for r in rows], axis=0)
    core = jnp.concatenate([core_ref[r, own] for r in rows], axis=0)
    gate = jnp.concatenate([gate_ref[r, cols] for r in rows], axis=0).astype(F32)
    core = core + mm(reach, state.astype(BF16))
    normed = core * lax.rsqrt(jnp.mean(core * core, axis=-1, keepdims=True) + 1e-6)
    return (normed * gain * (gate / (1.0 + jnp.exp(-gate)))).astype(BF16)


def part_rows(place_ref, share, offset, size):
    return [pl.ds(pl.multiple_of((i ^ place_ref[3]) * share + offset, 16), size) for i in range(4)]


def early_kernel(
    size, place_ref, reach_ref, core_ref, gate_ref, gain_ref, kept_ref, weight_ref, product_ref, gated_ref
):
    share = gate_ref.shape[0] // 4
    gain = gain_ref[...]
    half = kept_ref.shape[0]
    rows = part_rows(place_ref, share, 0, size)
    for j in range(half):
        own = slice(j * DV, (j + 1) * DV)
        cols = pl.ds(pl.multiple_of((place_ref[4] + j) * DV, DV), DV)
        gated_ref[:, own] = gated_rows(rows, own, cols, reach_ref, core_ref, gate_ref, gain, kept_ref[j])
    depth = half * DV
    product_ref[...] = mm(gated_ref[...], weight_ref[pl.ds(pl.multiple_of(place_ref[4] * DV, depth), depth), :])


def finish_kernel(offset, place_ref, reach_ref, core_ref, gate_ref, gain_ref, got_ref, weight_ref, *refs):
    gated_ref, (send_x_ref, send_y_ref, keep_l_ref, keep_r_ref) = refs[-1], refs[-5:-1]
    product_ref = refs[0] if len(refs) == 6 else None
    size = send_x_ref.shape[1]
    gain = gain_ref[...]
    half = got_ref.shape[0]
    depth = half * DV
    rows = part_rows(place_ref, gate_ref.shape[0] // 4, offset, size)
    for j in range(half):
        own = slice(j * DV, (j + 1) * DV)
        cols = pl.ds(pl.multiple_of((half - place_ref[4] + j) * DV, DV), DV)
        gated_ref[:, own] = gated_rows(rows, own, cols, reach_ref, core_ref, gate_ref, gain, got_ref[j])
    here = pl.ds(pl.multiple_of(place_ref[4] * DV, depth), depth)
    there = pl.ds(pl.multiple_of((half - place_ref[4]) * DV, depth), depth)
    if product_ref is None:
        early = []
        for j in range(half):
            own = slice(j * DV, (j + 1) * DV)
            cols = pl.ds(pl.multiple_of((place_ref[4] + j) * DV, DV), DV)
            early.append(gated_rows(rows, own, cols, refs[0], refs[1], gate_ref, gain, refs[2][j]))
        early = jnp.concatenate(early, axis=1)
    width = weight_ref.shape[1] // 2
    sums = []
    for cols in (slice(0, width), slice(width, 2 * width)):
        base = mm(early, weight_ref[here, cols]) if product_ref is None else product_ref[:, cols]
        sums.append(base + mm(gated_ref[...], weight_ref[there, cols]))
    left, right = sums
    for i, (l_ref, l_at, r_ref, r_at) in enumerate(
        (
            (keep_l_ref, 0, keep_r_ref, 0),
            (send_x_ref, 0, keep_r_ref, 1),
            (keep_l_ref, 1, send_y_ref, 0),
            (send_x_ref, 1, send_y_ref, 1),
        )
    ):
        l_ref[l_at] = left[i * size : (i + 1) * size]
        r_ref[r_at] = right[i * size : (i + 1) * size]


def begin(size, place, reads, gate, gain, kept, weight):
    tokens = gate.shape[0]
    local = pl.BlockSpec(memory_space=pltpu.VMEM)
    return pl.pallas_call(
        functools.partial(early_kernel, size),
        out_shape=jax.ShapeDtypeStruct((4 * size, weight.shape[1]), F32),
        in_specs=[pl.BlockSpec(memory_space=pltpu.SMEM)] + [local] * 6,
        out_specs=local,
        scratch_shapes=[pltpu.VMEM((4 * size, kept.shape[0] * DV), BF16)],
        compiler_params=pltpu.CompilerParams(vmem_limit_bytes=FINISH_VMEM),
        cost_estimate=pl.CostEstimate(flops=10**9, bytes_accessed=6 * 10**6, transcendentals=tokens * 512),
        name="early",
    )(place, *reads, gate, gain, kept, weight)


def finish(offset, size, place, reads, gate, gain, got, weight, early):
    width = weight.shape[1] // 2
    depth = got.shape[0] * DV
    local = pl.BlockSpec(memory_space=pltpu.VMEM)
    return pl.pallas_call(
        functools.partial(finish_kernel, offset),
        out_shape=[jax.ShapeDtypeStruct((2, size, width), F32)] * 4,
        in_specs=[pl.BlockSpec(memory_space=pltpu.SMEM)] + [local] * (6 + len(early)),
        out_specs=[local] * 4,
        scratch_shapes=[pltpu.VMEM((4 * size, depth), BF16)],
        compiler_params=pltpu.CompilerParams(vmem_limit_bytes=FINISH_VMEM),
        cost_estimate=pl.CostEstimate(
            flops=16 * size * depth * width * 2, bytes_accessed=16 * size * width, transcendentals=8 * size * depth
        ),
        name="finish",
    )(place, *reads, gate, gain, got, weight, *early)


def precise(left, right):
    return jnp.einsum("hij,hjk->hik", left, right, precision=lax.Precision.HIGHEST)


def combine(earlier, later):
    joined = precise(later[..., :DK], earlier)
    return jnp.concatenate([joined[..., :DK], joined[..., DK:] + later[..., DK:]], axis=-1)


def apply_map(pair, state):
    return precise(pair[..., :DK], state) + pair[..., DK:]


def group_hops(pair_map, pair_state, outer, beside=()):
    results, arrivals = [], []
    leaving = pair_state
    for hop in range(outer // 2):
        step = [(i, i + 1) for i in range(hop, outer - 1)] + [(outer - 1, hop)]
        state = lax.ppermute(leaving, "outer", step)
        if hop < len(beside):
            call, place, rest = beside[hop]
            place, _ = lax.optimization_barrier((place, leaving))
            result = call(place, *rest)
            state, result = lax.optimization_barrier((state, result))
            results.append(result)
        arrivals.append(state)
        if hop < outer // 2 - 1:
            if hop:
                state = jnp.where(lax.axis_index("outer") <= hop, arrivals[-2], state)
                arrivals[-1] = state
            leaving = precise(pair_map, state) + pair_state
    return arrivals[-2], arrivals[-1], results


def whole_prefix(mine, theirs, ctx, outer):
    here = lax.axis_index("ctx")
    both = jnp.concatenate([mine, theirs], axis=0)
    blocks = lax.all_gather(both, "ctx")
    identity = jnp.concatenate([jnp.eye(DK, dtype=F32), jnp.zeros((DK, DV), F32)], axis=1)
    start = jnp.broadcast_to(identity, both.shape)

    def hop(k, carry):
        before, through = carry
        through = combine(through, blocks[k])
        return jnp.where(k < here, through, before), through

    before, through = lax.fori_loop(0, ctx, hop, (start, start))
    former, latter, _ = group_hops(through[..., :DK], through[..., DK:], outer)
    entering = jnp.where(lax.axis_index("outer") < outer // 2, former, latter)
    state = apply_map(before, entering)
    half = mine.shape[0]
    return state[:half], state[half:]


def shards(ctx, outer, queries, keys, values, gate, decay, beta, docs, gain, weight):
    heads = decay.shape[0]
    here = lax.axis_index("ctx")
    position = lax.axis_index("outer") * ctx + here
    second = here if ctx == 2 else 0 * here
    group = lax.axis_index("outer")
    place = jnp.stack([1 - second, position, here, lax.axis_index("tp"), second * (heads // 2), group])
    place = place.astype(jnp.int32)
    lengths = lax.broadcast_in_dim(docs, (DOC_ROWS, docs.shape[0]), (1,))
    lengths = jnp.pad(lengths, ((0, 0), (0, decay.shape[1] - docs.shape[0]))).astype(F32)
    rates = jnp.concatenate([decay, beta, lengths], axis=0)
    theirs, mine, pair_t, pair_m, held_t, held_m, cum_t, cum_m = state_maps(place, keys, values, rates)
    if ctx == 2:
        swap = [(0, 1), (1, 0)]
        other = lax.ppermute(theirs, "ctx", swap)
        (group_state,) = small_call(functools.partial(group_kernel, slice(DK, DK + DV)), 1, place, mine, other)
        later, _ = lax.optimization_barrier((place, group_state))
        (group_map,) = small_call(functools.partial(group_kernel, slice(0, DK)), 1, later, mine, other)
        beside = (
            (functools.partial(read_out, 1), place, (queries, keys, cum_m, pair_m, held_m)),
            (functools.partial(read_out, 0), place, (queries, keys, cum_t, pair_t, held_t)),
        )
        former, latter, reads = group_hops(group_map, group_state, outer, beside)
        kept, sent = small_call(functools.partial(enter_kernel, outer // 2), 2, place, mine, other, former, latter)
        got = lax.ppermute(sent, "ctx", swap)
    else:
        kept, got = whole_prefix(mine, theirs, ctx, outer)
        reads = [
            read_out(1, place, queries, keys, cum_m, pair_m, held_m),
            read_out(0, place, queries, keys, cum_t, pair_t, held_t),
        ]
    gain = gain.reshape(1, DV)
    early_place = place
    if ctx == 2:
        early_place, _ = lax.optimization_barrier((place, sent))
    early = begin(PARTS[0], early_place, reads[0], gate, gain, kept, weight)
    along_x = [(i, i ^ 1) for i in range(4)]
    along_y = [(i, i ^ 2) for i in range(4)]
    halves, offset = [], 0
    for size in PARTS:
        send_x, send_y, keep_l, keep_r = finish(offset, size, place, reads[1], gate, gain, got, weight, (*reads[0], kept) if offset else (early,))
        offset += size
        got_x = lax.ppermute(send_x, "tp", along_x)
        got_y = lax.ppermute(send_y, "tp", along_y)
        halves.append((keep_l, keep_r, got_x, got_y))
    outs = []
    for keep_l, keep_r, got_x, got_y in halves:
        last_l = lax.ppermute(keep_l[1] + got_x[1], "tp", along_y)
        last_r = lax.ppermute(keep_r[1] + got_y[1], "tp", along_x)
        out_l = keep_l[0] + got_x[0] + last_l
        out_r = keep_r[0] + got_y[0] + last_r
        outs.append(jnp.concatenate([out_l, out_r], axis=1).astype(BF16))
    return jnp.concatenate(outs, axis=0)


def solution(mesh):
    ctx, outer = mesh.shape["ctx"], mesh.shape["outer"]
    in_specs = (
        P(("outer", "ctx"), "tp"),
        P(("outer", "ctx"), "tp"),
        P(("outer", "ctx"), "tp"),
        P(("outer", "ctx"), "tp"),
        P("tp", ("outer", "ctx")),
        P("tp", ("outer", "ctx")),
        P(),
        P(),
        P("tp", None),
    )
    out_specs = P(("outer", "ctx", "tp"), None)
    return jax.shard_map(
        functools.partial(shards, ctx, outer), mesh=mesh, in_specs=in_specs, out_specs=out_specs, check_vma=False
    )
```

```python
import functools

import jax
import jax.numpy as jnp
from jax import lax
from jax.experimental import pallas as pl
from jax.experimental.pallas import tpu as pltpu
from jax.sharding import PartitionSpec as P

DK = 128
DV = 128
STRETCH = 64
CHUNK = 2 * STRETCH
F32 = jnp.float32
BF16 = jnp.bfloat16
MIB = 1024 * 1024
MAPS_VMEM = 48 * MIB
READ_VMEM = 12 * MIB
SMALL_VMEM = 4 * MIB
FINISH_VMEM = 16 * MIB
PARTS = (32, 48, 48)
DOC_ROWS = 8
FAR = 1e30


def mm(left, right):
    return jnp.dot(left, right, preferred_element_type=F32)


def unit_rows(raw):
    raw = raw.astype(F32)
    return raw * lax.rsqrt(jnp.sum(raw * raw, axis=-1, keepdims=True) + 1e-6)


def corners(left, right):
    nil = jnp.zeros_like(left)
    return jnp.concatenate(
        [jnp.concatenate([left, nil], axis=1), jnp.concatenate([nil, right], axis=1)], axis=0
    )


def keep_flags(docs, first_stretch, stretches):
    before = lax.broadcasted_iota(jnp.int32, (CHUNK, CHUNK), 0) < lax.broadcasted_iota(jnp.int32, (CHUNK, CHUNK), 1)
    starts = mm(docs.astype(BF16), before.astype(F32).astype(BF16))[0:1, :]
    ids = (lax.broadcasted_iota(jnp.int32, (stretches, CHUNK), 0) + first_stretch).astype(F32)
    return 1.0 - jnp.max(jnp.where(ids == starts, 1.0, 0.0), axis=1, keepdims=True)


def fade_bias(row, col, k2):
    crossing = (row >= STRETCH) & (col < STRETCH)
    return jnp.where(row >= col, 0.0, -FAR) + jnp.where(crossing, (k2 - 1.0) * FAR, 0.0)


def maps_kernel(
    chunks, key_heads, place_ref, k_hbm, v_hbm, rates_hbm,
    theirs_ref, mine_ref, pair_t_ref, pair_m_ref, held_t_ref, held_m_ref, cum_t_ref, cum_m_ref,
    k_ref, v_ref, rates_ref, sems,
):
    half = key_heads // 2
    loads = [
        pltpu.make_async_copy(src, dst, sems.at[i])
        for i, (src, dst) in enumerate(
            (
                (rates_hbm, rates_ref),
                (k_hbm, k_ref),
                (v_hbm, v_ref),
            )
        )
    ]
    for load in loads:
        load.start()
    row = lax.broadcasted_iota(jnp.int32, (CHUNK, CHUNK), 0)
    col = lax.broadcasted_iota(jnp.int32, (CHUNK, CHUNK), 1)
    upper = (row <= col).astype(F32)
    eye = (row == col).astype(F32)
    below = (row > col).astype(F32)
    apart = row ^ col
    levels = CHUNK.bit_length() - 1
    masks = [((apart >> level) == 1).astype(F32).astype(BF16) for level in range(levels)]
    second = lax.broadcasted_iota(jnp.int32, (1, CHUNK), 1) >= STRETCH
    both_eye = jnp.concatenate([eye, eye], axis=1)
    loads[0].wait()
    heads_all = (rates_ref.shape[0] - DOC_ROWS) // 2
    keep = keep_flags(rates_ref[2 * heads_all :, :CHUNK], place_ref[1] * (2 * chunks), 2 * chunks)
    keeps = [(keep[2 * n : 2 * n + 1], keep[2 * n + 1 : 2 * n + 2]) for n in range(chunks)]
    loads[1].wait()

    outs = {}
    for step in range(2):
        side = lax.rem(step + place_ref[0], 2)
        turn = lax.rem(heads_all - 2 * half * side, heads_all)

        def by_chunk(first):
            rolled = pltpu.roll(rates_ref[first : first + heads_all, :], turn, 0)
            return jnp.concatenate(
                [rolled[:, n * CHUNK : (n + 1) * CHUNK] for n in range(chunks)], axis=0
            )

        decay, beta = by_chunk(0), by_chunk(heads_all)
        cum = jnp.dot(decay, upper, precision=lax.Precision.HIGHEST, preferred_element_type=F32)
        cum_ref = (cum_t_ref, cum_m_ref)[step]
        cum_ref[: chunks * heads_all, :] = cum
        cum_ref[chunks * heads_all :, :] = jnp.broadcast_to(keep, (2 * chunks, CHUNK))
        grown = jnp.exp(cum)
        cum_col, beta_col = cum.T, beta.T

        pairs = []
        for n in range(chunks):
            rows = slice(n * CHUNK, (n + 1) * CHUNK)
            k1, k2 = keeps[n]
            bias = fade_bias(row, col, k2)
            entry = jnp.where(second, k1 * k2, k1)
            leave = jnp.where(second, 1.0, k2)
            for g in range(half):
                key_cols = pl.ds(pl.multiple_of((side * half + g) * DK, DK), DK)
                k_unit = unit_rows(k_ref[rows, key_cols]).astype(BF16)
                k_turned = k_unit.astype(F32).T
                key_gram = mm(k_unit, k_turned.astype(BF16)) * below
                heads = []
                for e in range(2):
                    at = n * heads_all + 2 * g + e
                    c_row, c_col = cum[at : at + 1, :], cum_col[:, at : at + 1]
                    b_row = beta[at : at + 1, :]
                    fade = jnp.exp((c_col - c_row) + bias)
                    last = c_row[:, CHUNK - 1 : CHUNK]
                    heads.append(
                        dict(
                            noise=(key_gram * fade * beta_col[:, at : at + 1]).astype(BF16),
                            b_row=b_row,
                            be_row=b_row * grown[at : at + 1, :] * entry,
                            k_out=(k_turned * (jnp.exp(last - c_row) * leave)).astype(BF16),
                            through=jnp.exp(last) * (k1 * k2),
                        )
                    )
                pairs.append((n, g, k_unit, heads))

        inverses = [
            both_eye - jnp.concatenate([h["noise"] * masks[0] for h in heads], axis=1).astype(F32)
            for _, _, _, heads in pairs
        ]
        for level in range(1, levels):
            held = [t.astype(BF16) for t in inverses]
            part = [
                mm(t, corners(heads[0]["noise"] * masks[level], heads[1]["noise"] * masks[level])).astype(BF16)
                for t, (_, _, _, heads) in zip(held, pairs)
            ]
            inverses = [
                t - mm(p, corners(b[:, :CHUNK], b[:, CHUNK:])) for t, p, b in zip(inverses, part, held)
            ]

        if step == 0:
            loads[2].wait()
        pair_ref = (pair_t_ref, pair_m_ref)[step]
        for (n, g, k_unit, heads), t in zip(pairs, inverses):
            rows = slice(n * CHUNK, (n + 1) * CHUNK)
            values = v_ref[rows, pl.ds(pl.multiple_of((side * half + g) * 2 * DV, 2 * DV), 2 * DV)]
            b_rows = jnp.concatenate([h["b_row"] for h in heads], axis=1)
            wy_values = mm((t * b_rows).astype(BF16), corners(values[:, :DV], values[:, DV:])).astype(BF16)
            weighted = jnp.concatenate(
                [t[:, e * CHUNK : (e + 1) * CHUNK] * heads[e]["be_row"] for e in range(2)], axis=0
            )
            wy_keys = mm(weighted.astype(BF16), k_unit).astype(BF16)
            for e in range(2):
                pair = jnp.concatenate(
                    [wy_keys[e * CHUNK : (e + 1) * CHUNK], wy_values[:, e * DV : (e + 1) * DV]], axis=1
                )
                pair_ref[2 * g + e, rows, :] = pair
                outs[step, n, 2 * g + e] = (mm(heads[e]["k_out"], pair), heads[e]["through"])

    carried = {}
    for n in range(chunks):
        for step in range(2):
            for j in range(2 * half):
                moved, through = outs[step, n, j]
                if n == 0:
                    carried[step, j] = jnp.concatenate([eye * through - moved[:, :DK], moved[:, DK:]], axis=1)
                    continue
                held = carried[step, j].astype(BF16)
                (held_t_ref, held_m_ref)[step][j, n - 1] = held
                after = carried[step, j] * through - mm(moved[:, :DK].astype(BF16), held)
                carried[step, j] = jnp.concatenate([after[:, :DK], after[:, DK:] + moved[:, DK:]], axis=1)
    for j in range(2 * half):
        theirs_ref[j] = carried[0, j]
        mine_ref[j] = carried[1, j]


def state_maps(place, keys, values, rates):
    tokens, key_width = keys.shape
    key_heads = key_width // DK
    heads = (rates.shape[0] - DOC_ROWS) // 2
    chunks = tokens // CHUNK
    part = heads // 2
    local = pl.BlockSpec(memory_space=pltpu.VMEM)
    remote = pl.BlockSpec(memory_space=pltpu.HBM)
    return pl.pallas_call(
        functools.partial(maps_kernel, chunks, key_heads),
        out_shape=[jax.ShapeDtypeStruct((part, DK, DK + DV), F32)] * 2
        + [jax.ShapeDtypeStruct((part, tokens, DK + DV), BF16)] * 2
        + [jax.ShapeDtypeStruct((part, chunks - 1, DK, DK + DV), BF16)] * 2
        + [jax.ShapeDtypeStruct((chunks * (heads + 2), CHUNK), F32)] * 2,
        in_specs=[pl.BlockSpec(memory_space=pltpu.SMEM)] + [remote] * 3,
        out_specs=[local] * 8,
        scratch_shapes=[
            pltpu.VMEM(keys.shape, keys.dtype),
            pltpu.VMEM(values.shape, values.dtype),
            pltpu.VMEM(rates.shape, rates.dtype),
            pltpu.SemaphoreType.DMA((3,)),
        ],
        compiler_params=pltpu.CompilerParams(vmem_limit_bytes=MAPS_VMEM),
        name="state_maps",
    )(place, keys, values, rates)


def read_kernel(
    step, chunks, key_heads, place_ref, q_ref, k_ref, cum_ref, pair_ref, held_ref, reach_ref, core_ref
):
    half = key_heads // 2
    side = lax.rem(step + place_ref[0], 2)
    heads_all = 4 * half
    row = lax.broadcasted_iota(jnp.int32, (CHUNK, CHUNK), 0)
    col = lax.broadcasted_iota(jnp.int32, (CHUNK, CHUNK), 1)
    second_col = lax.broadcasted_iota(jnp.int32, (CHUNK, 1), 0) >= STRETCH
    keep = cum_ref[chunks * heads_all :, :]
    keeps = [(keep[2 * n : 2 * n + 1, 0:1], keep[2 * n + 1 : 2 * n + 2, 0:1]) for n in range(chunks)]
    cum = cum_ref[: chunks * heads_all, :]
    cum_col = cum.T
    grown_col = jnp.exp(cum_col)
    for n in range(chunks):
        rows = slice(n * CHUNK, (n + 1) * CHUNK)
        k1, k2 = keeps[n]
        bias = fade_bias(row, col, k2)
        entry_col = jnp.where(second_col, k1 * k2, k1)
        for g in range(half):
            key_cols = pl.ds(pl.multiple_of((side * half + g) * DK, DK), DK)
            k_unit = unit_rows(k_ref[rows, key_cols]).astype(BF16)
            q_unit = unit_rows(q_ref[rows, key_cols]).astype(BF16)
            query_gram = mm(q_unit, k_unit.astype(F32).T.astype(BF16))
            for e in range(2):
                j = 2 * g + e
                at = n * heads_all + j
                cols = slice(j * DV, (j + 1) * DV)
                fade = jnp.exp((cum_col[:, at : at + 1] - cum[at : at + 1, :]) + bias)
                seen = mm((query_gram * fade).astype(BF16), pair_ref[j, rows, :])
                q_in = q_unit.astype(F32) * (grown_col[:, at : at + 1] * entry_col)
                q_eff = (q_in - seen[:, :DK]).astype(BF16)
                if n == 0:
                    reach_ref[rows, cols] = q_eff
                    core_ref[rows, cols] = seen[:, DK:]
                else:
                    read = mm(q_eff, held_ref[j, n - 1])
                    reach_ref[rows, cols] = read[:, :DK].astype(BF16)
                    core_ref[rows, cols] = read[:, DK:] + seen[:, DK:]


def read_out(step, place, queries, keys, cum, pair, held):
    tokens, key_width = queries.shape
    key_heads = key_width // DK
    chunks = tokens // CHUNK
    local = pl.BlockSpec(memory_space=pltpu.VMEM)
    scalar = pl.BlockSpec(memory_space=pltpu.SMEM)
    width = pair.shape[0] * DV
    return pl.pallas_call(
        functools.partial(read_kernel, step, chunks, key_heads),
        out_shape=[
            jax.ShapeDtypeStruct((tokens, width), BF16),
            jax.ShapeDtypeStruct((tokens, width), F32),
        ],
        in_specs=[scalar] + [local] * 5,
        out_specs=[local] * 2,
        compiler_params=pltpu.CompilerParams(vmem_limit_bytes=READ_VMEM),
        cost_estimate=pl.CostEstimate(flops=2 * 10**9, bytes_accessed=6 * 10**6, transcendentals=10**6),
        name="read_out",
    )(place, queries, keys, cum, pair, held)


def two_terms(value):
    high = value.astype(BF16)
    return high, (value - high.astype(F32)).astype(BF16)


def exact(left, right):
    (high, low), (right_high, right_low) = two_terms(left), two_terms(right)
    rows = left.shape[0]
    both = mm(jnp.concatenate([high, low], axis=0), right_high)
    return both[:rows] + (both[rows:] + mm(high, right_low))


def group_kernel(columns, core_ref, mine_ref, other_ref, out_ref):
    def join(first_ref, second_ref):
        for j in range(first_ref.shape[0]):
            joined = exact(second_ref[j][:, :DK], first_ref[j][:, columns])
            out_ref[j] = joined + second_ref[j][:, DK:] if columns.start else joined

    @pl.when(core_ref[2] == 0)
    def _():
        join(mine_ref, other_ref)

    @pl.when(core_ref[2] == 1)
    def _():
        join(other_ref, mine_ref)


def enter_kernel(hops, core_ref, mine_ref, other_ref, former_ref, latter_ref, keep_ref, send_ref):
    early = core_ref[5] < hops

    def through(first_ref, same_ref, out_ref):
        for j in range(first_ref.shape[0]):
            state = jnp.where(early, former_ref[j], latter_ref[j])
            same_ref[j] = state
            out_ref[j] = exact(first_ref[j][:, :DK], state) + first_ref[j][:, DK:]

    @pl.when(core_ref[2] == 0)
    def _():
        through(mine_ref, keep_ref, send_ref)

    @pl.when(core_ref[2] == 1)
    def _():
        through(other_ref, send_ref, keep_ref)


def small_call(kernel, outs, place, *operands):
    part = operands[0].shape[0]
    local = pl.BlockSpec(memory_space=pltpu.VMEM)
    return pl.pallas_call(
        kernel,
        out_shape=[jax.ShapeDtypeStruct((part, DK, DV), F32)] * outs,
        in_specs=[pl.BlockSpec(memory_space=pltpu.SMEM)] + [local] * len(operands),
        out_specs=[local] * outs,
        compiler_params=pltpu.CompilerParams(vmem_limit_bytes=SMALL_VMEM),
    )(place, *operands)


def gated_rows(rows, own, cols, reach_ref, core_ref, gate_ref, gain, state):
    reach = jnp.concatenate([reach_ref[r, own] for r in rows], axis=0)
    core = jnp.concatenate([core_ref[r, own] for r in rows], axis=0)
    gate = jnp.concatenate([gate_ref[r, cols] for r in rows], axis=0).astype(F32)
    core = core + mm(reach, state.astype(BF16))
    normed = core * lax.rsqrt(jnp.mean(core * core, axis=-1, keepdims=True) + 1e-6)
    return (normed * gain * (gate / (1.0 + jnp.exp(-gate)))).astype(BF16)


def part_rows(place_ref, share, offset, size):
    return [pl.ds(pl.multiple_of((i ^ place_ref[3]) * share + offset, 16), size) for i in range(4)]


def early_kernel(
    size, place_ref, reach_ref, core_ref, gate_ref, gain_ref, kept_ref, weight_ref, product_ref, gated_ref
):
    share = gate_ref.shape[0] // 4
    gain = gain_ref[...]
    half = kept_ref.shape[0]
    rows = part_rows(place_ref, share, 0, size)
    for j in range(half):
        own = slice(j * DV, (j + 1) * DV)
        cols = pl.ds(pl.multiple_of((place_ref[4] + j) * DV, DV), DV)
        gated_ref[:, own] = gated_rows(rows, own, cols, reach_ref, core_ref, gate_ref, gain, kept_ref[j])
    depth = half * DV
    product_ref[...] = mm(gated_ref[...], weight_ref[pl.ds(pl.multiple_of(place_ref[4] * DV, depth), depth), :])


def finish_kernel(offset, place_ref, reach_ref, core_ref, gate_ref, gain_ref, got_ref, weight_ref, *refs):
    gated_ref, (send_x_ref, send_y_ref, keep_l_ref, keep_r_ref) = refs[-1], refs[-5:-1]
    product_ref = refs[0] if len(refs) == 6 else None
    size = send_x_ref.shape[1]
    gain = gain_ref[...]
    half = got_ref.shape[0]
    depth = half * DV
    rows = part_rows(place_ref, gate_ref.shape[0] // 4, offset, size)
    for j in range(half):
        own = slice(j * DV, (j + 1) * DV)
        cols = pl.ds(pl.multiple_of((half - place_ref[4] + j) * DV, DV), DV)
        gated_ref[:, own] = gated_rows(rows, own, cols, reach_ref, core_ref, gate_ref, gain, got_ref[j])
    here = pl.ds(pl.multiple_of(place_ref[4] * DV, depth), depth)
    there = pl.ds(pl.multiple_of((half - place_ref[4]) * DV, depth), depth)
    if product_ref is None:
        early = []
        for j in range(half):
            own = slice(j * DV, (j + 1) * DV)
            cols = pl.ds(pl.multiple_of((place_ref[4] + j) * DV, DV), DV)
            early.append(gated_rows(rows, own, cols, refs[0], refs[1], gate_ref, gain, refs[2][j]))
        early = jnp.concatenate(early, axis=1)
    width = weight_ref.shape[1] // 2
    sums = []
    for cols in (slice(0, width), slice(width, 2 * width)):
        base = mm(early, weight_ref[here, cols]) if product_ref is None else product_ref[:, cols]
        sums.append(base + mm(gated_ref[...], weight_ref[there, cols]))
    left, right = sums
    for i, (l_ref, l_at, r_ref, r_at) in enumerate(
        (
            (keep_l_ref, 0, keep_r_ref, 0),
            (send_x_ref, 0, keep_r_ref, 1),
            (keep_l_ref, 1, send_y_ref, 0),
            (send_x_ref, 1, send_y_ref, 1),
        )
    ):
        l_ref[l_at] = left[i * size : (i + 1) * size]
        r_ref[r_at] = right[i * size : (i + 1) * size]


def begin(size, place, reads, gate, gain, kept, weight):
    tokens = gate.shape[0]
    local = pl.BlockSpec(memory_space=pltpu.VMEM)
    return pl.pallas_call(
        functools.partial(early_kernel, size),
        out_shape=jax.ShapeDtypeStruct((4 * size, weight.shape[1]), F32),
        in_specs=[pl.BlockSpec(memory_space=pltpu.SMEM)] + [local] * 6,
        out_specs=local,
        scratch_shapes=[pltpu.VMEM((4 * size, kept.shape[0] * DV), BF16)],
        compiler_params=pltpu.CompilerParams(vmem_limit_bytes=FINISH_VMEM),
        cost_estimate=pl.CostEstimate(flops=10**9, bytes_accessed=6 * 10**6, transcendentals=tokens * 512),
        name="early",
    )(place, *reads, gate, gain, kept, weight)


def finish(offset, size, place, reads, gate, gain, got, weight, early):
    width = weight.shape[1] // 2
    depth = got.shape[0] * DV
    local = pl.BlockSpec(memory_space=pltpu.VMEM)
    return pl.pallas_call(
        functools.partial(finish_kernel, offset),
        out_shape=[jax.ShapeDtypeStruct((2, size, width), F32)] * 4,
        in_specs=[pl.BlockSpec(memory_space=pltpu.SMEM)] + [local] * (6 + len(early)),
        out_specs=[local] * 4,
        scratch_shapes=[pltpu.VMEM((4 * size, depth), BF16)],
        compiler_params=pltpu.CompilerParams(vmem_limit_bytes=FINISH_VMEM),
        cost_estimate=pl.CostEstimate(
            flops=16 * size * depth * width * 2, bytes_accessed=16 * size * width, transcendentals=8 * size * depth
        ),
        name="finish",
    )(place, *reads, gate, gain, got, weight, *early)


def precise(left, right):
    return jnp.einsum("hij,hjk->hik", left, right, precision=lax.Precision.HIGH)


def combine(earlier, later):
    joined = precise(later[..., :DK], earlier)
    return jnp.concatenate([joined[..., :DK], joined[..., DK:] + later[..., DK:]], axis=-1)


def apply_map(pair, state):
    return precise(pair[..., :DK], state) + pair[..., DK:]


def group_hops(pair_map, pair_state, outer, beside=()):
    results, arrivals = [], []
    leaving = pair_state
    for hop in range(outer // 2):
        step = [(i, i + 1) for i in range(hop, outer - 1)] + [(outer - 1, hop)]
        state = lax.ppermute(leaving, "outer", step)
        if hop < len(beside):
            call, place, rest = beside[hop]
            place, _ = lax.optimization_barrier((place, leaving))
            result = call(place, *rest)
            state, result = lax.optimization_barrier((state, result))
            results.append(result)
        arrivals.append(state)
        if hop < outer // 2 - 1:
            if hop:
                state = jnp.where(lax.axis_index("outer") <= hop, arrivals[-2], state)
                arrivals[-1] = state
            leaving = precise(pair_map, state) + pair_state
    return arrivals[-2], arrivals[-1], results


def whole_prefix(mine, theirs, ctx, outer):
    here = lax.axis_index("ctx")
    both = jnp.concatenate([mine, theirs], axis=0)
    blocks = lax.all_gather(both, "ctx")
    identity = jnp.concatenate([jnp.eye(DK, dtype=F32), jnp.zeros((DK, DV), F32)], axis=1)
    start = jnp.broadcast_to(identity, both.shape)

    def hop(k, carry):
        before, through = carry
        through = combine(through, blocks[k])
        return jnp.where(k < here, through, before), through

    before, through = lax.fori_loop(0, ctx, hop, (start, start))
    former, latter, _ = group_hops(through[..., :DK], through[..., DK:], outer)
    entering = jnp.where(lax.axis_index("outer") < outer // 2, former, latter)
    state = apply_map(before, entering)
    half = mine.shape[0]
    return state[:half], state[half:]


def shards(ctx, outer, queries, keys, values, gate, decay, beta, docs, gain, weight):
    heads = decay.shape[0]
    here = lax.axis_index("ctx")
    position = lax.axis_index("outer") * ctx + here
    second = here if ctx == 2 else 0 * here
    group = lax.axis_index("outer")
    place = jnp.stack([1 - second, position, here, lax.axis_index("tp"), second * (heads // 2), group])
    place = place.astype(jnp.int32)
    lengths = lax.broadcast_in_dim(docs, (DOC_ROWS, docs.shape[0]), (1,))
    lengths = jnp.pad(lengths, ((0, 0), (0, decay.shape[1] - docs.shape[0]))).astype(F32)
    rates = jnp.concatenate([decay, beta, lengths], axis=0)
    theirs, mine, pair_t, pair_m, held_t, held_m, cum_t, cum_m = state_maps(place, keys, values, rates)
    if ctx == 2:
        swap = [(0, 1), (1, 0)]
        other = lax.ppermute(theirs, "ctx", swap)
        (group_state,) = small_call(functools.partial(group_kernel, slice(DK, DK + DV)), 1, place, mine, other)
        later, _ = lax.optimization_barrier((place, group_state))
        (group_map,) = small_call(functools.partial(group_kernel, slice(0, DK)), 1, later, mine, other)
        beside = (
            (functools.partial(read_out, 1), place, (queries, keys, cum_m, pair_m, held_m)),
            (functools.partial(read_out, 0), place, (queries, keys, cum_t, pair_t, held_t)),
        )
        former, latter, reads = group_hops(group_map, group_state, outer, beside)
        kept, sent = small_call(functools.partial(enter_kernel, outer // 2), 2, place, mine, other, former, latter)
        got = lax.ppermute(sent, "ctx", swap)
    else:
        kept, got = whole_prefix(mine, theirs, ctx, outer)
        reads = [
            read_out(1, place, queries, keys, cum_m, pair_m, held_m),
            read_out(0, place, queries, keys, cum_t, pair_t, held_t),
        ]
    gain = gain.reshape(1, DV)
    early_place = place
    if ctx == 2:
        early_place, _ = lax.optimization_barrier((place, sent))
    early = begin(PARTS[0], early_place, reads[0], gate, gain, kept, weight)
    along_x = [(i, i ^ 1) for i in range(4)]
    along_y = [(i, i ^ 2) for i in range(4)]
    halves, offset = [], 0
    for size in PARTS:
        send_x, send_y, keep_l, keep_r = finish(offset, size, place, reads[1], gate, gain, got, weight, (*reads[0], kept) if offset else (early,))
        offset += size
        got_x = lax.ppermute(send_x, "tp", along_x)
        got_y = lax.ppermute(send_y, "tp", along_y)
        halves.append((keep_l, keep_r, got_x, got_y))
    outs = []
    for keep_l, keep_r, got_x, got_y in halves:
        last_l = lax.ppermute(keep_l[1] + got_x[1], "tp", along_y)
        last_r = lax.ppermute(keep_r[1] + got_y[1], "tp", along_x)
        out_l = keep_l[0] + got_x[0] + last_l
        out_r = keep_r[0] + got_y[0] + last_r
        outs.append(jnp.concatenate([out_l, out_r], axis=1).astype(BF16))
    return jnp.concatenate(outs, axis=0)


def solution(mesh):
    ctx, outer = mesh.shape["ctx"], mesh.shape["outer"]
    in_specs = (
        P(("outer", "ctx"), "tp"),
        P(("outer", "ctx"), "tp"),
        P(("outer", "ctx"), "tp"),
        P(("outer", "ctx"), "tp"),
        P("tp", ("outer", "ctx")),
        P("tp", ("outer", "ctx")),
        P(),
        P(),
        P("tp", None),
    )
    out_specs = P(("outer", "ctx", "tp"), None)
    return jax.shard_map(
        functools.partial(shards, ctx, outer), mesh=mesh, in_specs=in_specs, out_specs=out_specs, check_vma=False
    )
```
